256 devices in a mesh: smp: 4 (over z_lo), qry: 32 (over y, z_hi, x), key: 2 (over core).
Axes of the slice: x: 4, y: 4, z: 8 (z_hi: 2, z_lo: 4; z = z_hi * 4 + z_lo), core: 2. Of those that a mesh axis runs over, the one named last changes fastest.
Arguments:
- query_proj: bfloat16 [2048, 8, 768], P('qry', 'smp', 'key'), may hold values from -6 to 6
- key_proj: bfloat16 [2048, 8, 768], P('qry', 'smp', 'key'), may hold values from -6 to 6
- value_proj: bfloat16 [2048, 8, 768], P('qry', 'smp', 'key'), may hold values from -6 to 6
- grad_out: bfloat16 [2048, 8, 768], P('qry', 'smp', 'key'), may hold values from -24 to 24
- pair_feats: bfloat16 [2048, 2048, 128], P('qry', ('smp', 'key')), may hold values from -400 to 400
- pair_gain: float32 [128], replicated, may hold values from 0.1 to 1.9
- bias_weight: bfloat16 [128, 16], replicated, may hold values from -0.5 to 0.5
- atom_counts: int32 [2048], replicated, may hold values from 0 to 23, as said below
Outputs:
- query_grad: bfloat16 [2048, 8, 768], P('qry', 'smp', 'key')
- key_grad: bfloat16 [2048, 8, 768], P('qry', 'smp', 'key')
- value_grad: bfloat16 [2048, 8, 768], P('qry', 'smp', 'key')
- weight_grad: float32 [128, 16], replicated
- gain_grad: float32 [128], replicated
The draws below stay inside these ranges and needn't reach their ends.
Inputs may be any that keep to these rules, and one draw needn't show every extreme that they name: `atom_counts`: tokens without atoms are padding and form a suffix of 256 to 512 tokens.
All inputs are finite; a program needn't handle non-finite values.
Results may differ from the reference program's by a relative error of at most 0.015.
Values may be sent and summed in bfloat16 or wider, within the bound.
A program may use at most 128 MiB of HBM per device.

```python
import math
import jax
import jax.numpy as jnp
from jax import lax

D = 768
H = 16
CZ = 128
TOK_DEV = 64
DH = 48
TOKENS = 2048
SAMPLES = 8
N_QRY = 32


def draw_query_proj(key, part):
    source = jax.random.fold_in(key, 1)
    return jnp.clip(jax.random.normal(source, (TOKENS, SAMPLES, D), jnp.float32), -4.0, 4.0).astype(jnp.bfloat16)


def draw_key_proj(key, part):
    source = jax.random.fold_in(key, 2)
    return jnp.clip(jax.random.normal(source, (TOKENS, SAMPLES, D), jnp.float32), -4.0, 4.0).astype(jnp.bfloat16)


def draw_pair_feats(key, part):
    key = jax.random.fold_in(key, 7)
    subkeys = jax.random.split(key, 3)
    channel = jnp.exp(jax.random.uniform(subkeys[0], (CZ,), jnp.float32, 0.0, math.log(10.0)))
    scaling = jnp.exp(jax.random.uniform(subkeys[1], (TOKENS, TOKENS, 1), jnp.float32, 0.0, math.log(10.0)))
    entries = jnp.clip(jax.random.normal(subkeys[2], (TOKENS, TOKENS, CZ), jnp.float32), -4.0, 4.0)
    return (entries * channel * scaling).astype(jnp.bfloat16)


def draw_atom_counts(key, part):
    key = jax.random.fold_in(key, 13)
    subkeys = jax.random.split(key, 2)
    padding = jax.random.randint(subkeys[0], (), TOKENS // 8, TOKENS // 4 + 1)
    counts = jax.random.randint(subkeys[1], (TOKENS,), 1, 24)
    position = jnp.arange(TOKENS, dtype=jnp.int32)
    return jnp.where(position >= TOKENS - padding, 0, counts).astype(jnp.int32)


def block_levels(own_key, extent, cuts, least, largest):
    def one(dim, blocks):
        heights = jax.random.uniform(jax.random.fold_in(jax.random.fold_in(own_key, 6), dim), (blocks,), jnp.float32, least / len(cuts), largest / len(cuts))
        return jnp.repeat(jnp.exp(heights), extent[dim] // blocks).reshape((-1,) + (1,) * (len(extent) - dim - 1))

    factor_of = one(*cuts[0])
    for cut in cuts[1:]:
        factor_of = factor_of * one(*cut)
    return factor_of


def noise(key, extent, width, limit, cuts=(), held_as=jnp.bfloat16):
    level = block_levels(key, extent, cuts, -0.22, 0.18) if cuts else 1.0
    drawn = jax.random.normal(key, extent, jnp.float32) * width * level
    return jnp.minimum(jnp.maximum(drawn, -limit), limit).astype(held_as)


def setup_inputs(seed: int = 0) -> dict:
    arg_keys = jax.random.split(jax.random.key(seed), 9)
    return {
        "query_proj": draw_query_proj(jax.random.fold_in(arg_keys[8], 71), 0),
        "key_proj": draw_key_proj(jax.random.fold_in(arg_keys[8], 71), 0),
        "value_proj": noise(arg_keys[2], (TOKENS, SAMPLES, D), 1.0, 6.0, ((0, 32), (1, 4), (2, 2))),
        "grad_out": noise(arg_keys[3], (TOKENS, SAMPLES, D), 4.0, 24.0, ((0, 32), (1, 4), (2, 2))),
        "pair_feats": draw_pair_feats(jax.random.fold_in(arg_keys[8], 71), 0),
        "pair_gain": jnp.clip(1.0 + 0.18 * jax.random.normal(arg_keys[5], (CZ,), jnp.float32), 0.1, 1.9),
        "bias_weight": noise(arg_keys[6], (CZ, H), CZ ** -0.5, 0.5),
        "atom_counts": draw_atom_counts(jax.random.fold_in(arg_keys[8], 71), 0),
    }


def rounded(values):
    return lax.optimization_barrier(values.astype(jnp.bfloat16)).astype(jnp.float32)

def layer_normed(tile_rows):
    values = tile_rows.astype(jnp.float32)
    center = values - lax.optimization_barrier(jnp.mean(values, axis=-1, keepdims=True))
    spread = lax.optimization_barrier(jnp.mean(center * center, axis=-1, keepdims=True))
    return center * lax.rsqrt(spread + 1e-05)

def reference(query_proj, key_proj, value_proj, grad_out, pair_feats, pair_gain, bias_weight, atom_counts):
    factor = DH ** (-0.5)
    highest = lax.Precision.HIGHEST
    weight_wide = bias_weight.astype(jnp.float32)
    blocks = pair_feats.reshape(N_QRY, TOK_DEV, TOKENS, CZ)

    def block_bias(tile_rows):
        normed = layer_normed(tile_rows) * pair_gain
        return jnp.einsum('rjc,ch->hrj', normed, weight_wide, precision=highest).astype(jnp.bfloat16)
    bias_all = jnp.moveaxis(lax.map(block_bias, blocks), 1, 0).reshape(H, TOKENS, TOKENS)
    bias_wide = lax.optimization_barrier(bias_all).astype(jnp.float32)
    usable = atom_counts > 0

    def sample_step(carry, inputs):
        query_rows = inputs[0].astype(jnp.float32).reshape(TOKENS, H, DH)
        key_rows = inputs[1].astype(jnp.float32).reshape(TOKENS, H, DH)
        value_rows = inputs[2].astype(jnp.float32).reshape(TOKENS, H, DH)
        grad_rows = inputs[3].astype(jnp.float32).reshape(TOKENS, H, DH)
        scores = jnp.einsum('ihd,jhd->hij', query_rows, key_rows, precision=highest) * factor + bias_wide
        scores = jnp.where(usable, scores, -jnp.inf)
        exponent = jnp.exp(scores - lax.optimization_barrier(jnp.max(scores, axis=-1, keepdims=True)))
        weights = exponent / lax.optimization_barrier(jnp.sum(exponent, axis=-1, keepdims=True))
        slopes = jnp.einsum('ihd,jhd->hij', grad_rows, value_rows, precision=highest)
        centred = lax.optimization_barrier(jnp.sum(weights * slopes, axis=-1, keepdims=True))
        score_grad = weights * (slopes - centred)
        score_low = rounded(score_grad)
        weights_low = rounded(weights)
        query_grad = (jnp.einsum('hij,jhd->ihd', score_low, key_rows, precision=highest) * factor).astype(jnp.bfloat16)
        key_grad = (jnp.einsum('hij,ihd->jhd', score_low, query_rows, precision=highest) * factor).astype(jnp.bfloat16)
        value_grad = jnp.einsum('hij,ihd->jhd', weights_low, grad_rows, precision=highest).astype(jnp.bfloat16)
        return (carry + score_grad, (query_grad.reshape(TOKENS, D), key_grad.reshape(TOKENS, D), value_grad.reshape(TOKENS, D)))
    inputs = (jnp.swapaxes(query_proj, 0, 1), jnp.swapaxes(key_proj, 0, 1), jnp.swapaxes(value_proj, 0, 1), jnp.swapaxes(grad_out, 0, 1))
    initial = jnp.zeros((H, TOKENS, TOKENS), jnp.float32)
    bias_grad, outputs = lax.scan(sample_step, initial, inputs)
    query_grad = jnp.swapaxes(outputs[0], 0, 1)
    key_grad = jnp.swapaxes(outputs[1], 0, 1)
    value_grad = jnp.swapaxes(outputs[2], 0, 1)
    grad_blocks = jnp.moveaxis(bias_grad.reshape(H, N_QRY, TOK_DEV, TOKENS), 1, 0)

    def block_weight(pieces):
        return jnp.einsum('rjc,hrj->ch', layer_normed(pieces[0]), pieces[1], precision=highest)
    summed = lax.optimization_barrier(jnp.sum(lax.map(block_weight, (blocks, grad_blocks)), axis=0))
    weight_grad = pair_gain[:, None] * summed
    gain_grad = lax.optimization_barrier(jnp.sum(summed * weight_wide, axis=1))
    return (query_grad, key_grad, value_grad, weight_grad, gain_grad)
```

```python
import jax
import jax.numpy as jnp
from jax import lax
from jax.experimental import pallas as pl
from jax.experimental.pallas import tpu as pltpu
from jax.sharding import PartitionSpec as P

DH = 48
HEADS = 16
TOKENS = 2048
LIVE = 1792
ROWS = 128
CHUNKS = 4
PAIRS = 14
FACTOR = DH ** (-0.5)
LOG2E = 1.4426950408889634
MESH = pl.DeviceIdType.MESH
F32 = jnp.float32
BF16 = jnp.bfloat16


def rem(a, b):
    return lax.rem(a, jnp.int32(b))


def div(a, b):
    return lax.div(a, jnp.int32(b))


def dot(a, b):
    return jnp.dot(a, b, preferred_element_type=F32)


def dot_nt(a, b):
    return lax.dot_general(a, b, (((1,), (1,)), ((), ())), preferred_element_type=F32)


def wait_bytes(ref, sem):
    pltpu.make_async_copy(ref, ref, sem).wait()


def kernel(
    a_ref, x_ref, wt_ref, gain_ref, ac_ref,
    o_ref, wg_ref, gg_ref,
    n_ref, skv, sqd, g_ref, r_ref, bsf, bs, br, bf,
    kvt, qdt, s_ref, p_ref, w_ref, ds_ref, db, dkv, dq, d_ref, qb,
    h1, f1, h2, f2, fb, ob, dbs, dr, df, ra, rb,
    x_sem, kv_send, kv_recv, qd_sem, bias_sem, ag_send, ag_recv,
    rs_send, rs_recv, ob_sem, db_sem, ar_sem,
):
    smp = lax.axis_index("smp")
    qry = lax.axis_index("qry")
    key = lax.axis_index("key")
    y = div(qry, 8)
    zh = rem(div(qry, 4), 2)
    x = rem(qry, 4)
    z = zh * 4 + smp
    cidx = smp * 2 + key
    head = key * 8 + z
    live_cols = cidx < 7

    def dev(xx, yy, zz, kk):
        return (rem(zz, 4), yy * 8 + div(zz, 4) * 4 + xx, kk)

    def rcopy(src, dst, send, recv, device):
        return pltpu.make_async_remote_copy(
            src_ref=src, dst_ref=dst, send_sem=send, recv_sem=recv, device_id=device, device_id_type=MESH
        )

    def zline():
        for dz in range(8):
            for dk in range(2):
                yield dz, dk, rem(z + dz, 8), rem(key + dk, 2)

    x_copies = [
        pltpu.make_async_copy(x_ref.at[pl.ds(16 * rc, 16)], n_ref.at[pl.ds(16 * rc, 16)], x_sem.at[rc])
        for rc in range(4)
    ]
    for copy in x_copies:
        copy.start()

    barrier = pltpu.get_barrier_semaphore()
    for dz, dk, zz, kk in zline():
        if dz or dk:
            pl.semaphore_signal(barrier, inc=1, device_id=dev(x, y, zz, kk), device_id_type=MESH)
    for dy in range(4):
        for dx in range(4):
            if dy or dx:
                pl.semaphore_signal(
                    barrier, inc=1, device_id=dev(rem(x + dx, 4), rem(y + dy, 4), z, key), device_id_type=MESH
                )

    for a in range(4):
        turned = a_ref[a].astype(F32).T.astype(BF16).reshape(8, DH, 128)
        if a < 2:
            skv[:, a] = turned
        else:
            sqd[:, a - 2] = turned

    db[...] = jnp.zeros_like(db)
    for c in range(CHUNKS):
        d_ref[c, 3, :, 1] = jnp.zeros((4, 2, DH, 128), BF16)

    pl.semaphore_wait(barrier, 30)

    for dz in range(8):
        zz = rem(z + dz, 8)
        dst = g_ref.at[smp, y, x, zh]
        if dz == 0:
            pltpu.make_async_copy(skv.at[zz], dst, kv_recv.at[smp]).start()
        else:
            rcopy(skv.at[zz], dst, kv_send, kv_recv.at[smp], dev(x, y, zz, key)).start()
    for dz in range(8):
        zz = rem(z + dz, 8)
        dst = r_ref.at[smp, zh]
        if dz == 0:
            pltpu.make_async_copy(sqd.at[zz], dst, qd_sem.at[1]).start()
        else:
            rcopy(sqd.at[zz], dst, qd_sem.at[0], qd_sem.at[1], dev(x, y, zz, key)).start()

    gw = wt_ref[...] * gain_ref[...]
    gw_high = gw.astype(BF16)
    gw_low = (gw - gw_high.astype(F32)).astype(BF16)
    gw_both = jnp.concatenate([gw_high, gw_low], axis=0)
    mean_of = jnp.full((128, 128), 1.0 / 128, BF16)

    def bias_rows(rc):
        x_copies[rc].wait()

        def step(i, carry):
            row = rc * 16 + 2 * i
            tile = n_ref[pl.ds(row, 2)].reshape(512, 128)
            center = tile.astype(F32) - dot(tile, mean_of)
            square = center * center
            high = square.astype(BF16)
            low = (square - high.astype(F32)).astype(BF16)
            spread = dot(high, mean_of) + dot(low, mean_of)
            normed = (center * lax.rsqrt(spread + 1e-05)).astype(BF16)
            n_ref[pl.ds(row, 2)] = normed.reshape(2, 256, 128)
            out = dot_nt(gw_both, normed)
            out = out[:16] + out[16:]
            for j in range(2):
                for half in range(2):
                    bsf[half, pl.ds((2 * i + j) * 16, 16)] = out[:, j * 256 + half * 128 : j * 256 + half * 128 + 128]
            return carry

        lax.fori_loop(0, 8, step, 0)
        for h in range(16):
            pieces = [bsf[half, pl.ds(h, 16, stride=16)] for half in range(2)]
            bs[rc, h] = jnp.concatenate(pieces, axis=1).astype(BF16)

        @pl.when(live_cols)
        def _():
            dst = br.at[pl.ds(zh * 64 + 16 * rc, 16), pl.ds(pl.multiple_of(cidx * 256, 256), 256)]
            for dz, dk, zz, kk in zline():
                src = bs.at[rc, kk * 8 + zz]
                if dz or dk:
                    rcopy(src, dst, bias_sem.at[0], bias_sem.at[1], dev(x, y, zz, kk)).start()
                else:
                    pltpu.make_async_copy(src, dst, bias_sem.at[1]).start()

    def spot(c, dp, dq):
        dx, dy = (dp, dq) if c % 2 == 0 else (dq, dp)
        return rem(x + dx + 4, 4), rem(y + dy + 4, 4)

    def there(c, dp, dq):
        xx, yy = spot(c, dp, dq)
        return dev(xx, yy, z, key)

    def block(c, dp, dq):
        xx, yy = spot(c, dp, dq)
        return (c, yy, xx)

    def gather_send(c, where, half, sem, target):
        src = g_ref.at[where] if half is None else g_ref.at[where + (half,)]
        rcopy(src, src, ag_send.at[c, sem], ag_recv.at[where + (half or 0,)], target).start()

    def gather_wait(where, half):
        ref = g_ref.at[where] if half is None else g_ref.at[where + (half,)]
        wait_bytes(ref, ag_recv.at[where + (half or 0,)])

    def gather_1(c):
        wait_bytes(g_ref.at[c, y, x], kv_recv.at[c])
        for d in (1, -1):
            gather_send(c, block(c, 0, 0), None, 0, there(c, d, 0))

    def gather_2(c):
        for d in (1, -1):
            gather_send(c, block(c, 0, 0), None, 1, there(c, 0, d))
        for half, d in ((0, 1), (1, -1)):
            where = block(c, -d, 0)
            gather_wait(where, None)
            gather_send(c, where, half, 3, there(c, d, 0))
            for e in (1, -1):
                gather_send(c, where, None, 1, there(c, 0, e))

    def gather_3(c):
        where = block(c, 2, 0)
        for half in range(2):
            gather_wait(where, half)
        for e in (1, -1):
            gather_send(c, where, None, 0, there(c, 0, e))

    def gather_4(c):
        for dp in (0, -1, 1, 2):
            for half, e in ((0, 1), (1, -1)):
                where = block(c, dp, -e)
                gather_wait(where, None)
                gather_send(c, where, half, 2, there(c, 0, e))

    def gather_5(c):
        for dp in (0, -1, 1, 2):
            for half in range(2):
                gather_wait(block(c, dp, 2), half)

    def gather_end(c):
        wait_bytes(g_ref.at[c, 0], ag_send.at[c, 0])
        wait_bytes(g_ref.at[c, pl.ds(0, 3), pl.ds(0, 2)], ag_send.at[c, 1])
        wait_bytes(g_ref.at[c, 0], ag_send.at[c, 2])
        wait_bytes(g_ref.at[c, 0, 0], ag_send.at[c, 3])

    low_lanes = lax.broadcasted_iota(jnp.int32, (DH, 128), 1) < 64

    def merge(first, second):
        return (
            jnp.where(low_lanes, first, pltpu.roll(second, 64, 1)),
            jnp.where(low_lanes, pltpu.roll(first, 64, 1), second),
        )

    def attention(c):
        for yy in range(4):
            for hi in range(2):
                if yy == 3 and hi == 1:
                    continue
                for m in range(2):
                    tile = yy * 4 + hi * 2 + m
                    for a in range(2):
                        both = merge(
                            g_ref[c, yy, 2 * m, hi, a].astype(F32), g_ref[c, yy, 2 * m + 1, hi, a].astype(F32)
                        )
                        for par in range(2):
                            kvt[par, a, :, tile * 128 : tile * 128 + 128] = both[par].astype(BF16)
        for a in range(2):
            both = merge(r_ref[c, 0, a].astype(F32), r_ref[c, 1, a].astype(F32))
            for par in range(2):
                qdt[par, a] = both[par].astype(BF16)

        def one(par, carry):
            query_t, grad_t = qdt[par, 0], qdt[par, 1]
            query = query_t.astype(F32).T.astype(BF16)
            grad = grad_t.astype(F32).T.astype(BF16)
            keys_t, values_t = kvt[par, 0], kvt[par, 1]
            s_ref[...] = dot(query, keys_t)
            p_ref[...] = dot(grad, values_t)

            def rows(g, inner):
                at = pl.ds(pl.multiple_of(g * 16, 16), 16)
                scores = s_ref[at] * (FACTOR * LOG2E) + bf[at]
                top = jnp.max(scores, axis=1, keepdims=True)
                exponent = jnp.exp2(scores - top)
                slopes = p_ref[at]
                total = jnp.sum(exponent, axis=1, keepdims=True)
                mixed = jnp.sum(exponent * slopes, axis=1, keepdims=True)
                inverse = 1.0 / total
                weights = exponent * inverse
                score_grad = weights * (slopes - mixed * inverse)
                w_ref[at] = weights.astype(BF16)
                ds_ref[at] = score_grad.astype(BF16)
                db[at] += score_grad
                return inner

            lax.fori_loop(0, 8, rows, 0)
            dkv[par, 0] = dot(query_t, ds_ref[...])
            dkv[par, 1] = dot(grad_t, w_ref[...])
            dq[par] = dot_nt(keys_t, ds_ref[...]) * FACTOR
            return carry

        lax.fori_loop(0, 2, one, 0)
        for yy in range(4):
            for hi in range(2):
                if yy == 3 and hi == 1:
                    continue
                for m in range(2):
                    tile = yy * 4 + hi * 2 + m
                    for a in range(2):
                        lanes = slice(tile * 128, tile * 128 + 128)
                        both = merge(dkv[0, a, :, lanes], dkv[1, a, :, lanes])
                        for e in range(2):
                            d_ref[c, yy, 2 * m + e, hi, a] = both[e].astype(BF16)
        both = merge(dq[0], dq[1])
        for hi in range(2):
            qb[c, hi] = both[hi].astype(BF16)

    def line(c, dp, half=None):
        xx, yy = spot(c, dp, 0)
        ref = d_ref.at[c, :, xx] if c % 2 == 0 else d_ref.at[c, yy]
        return ref if half is None else ref.at[:, half]

    def home(c, dq):
        return d_ref.at[block(c, 0, dq)]

    def plus(ref, *others):
        total = ref[...].astype(F32)
        for other in others:
            total += other[...].astype(F32)
        return total

    def reduce_1(c):
        for half, d in ((0, 1), (1, -1)):
            rcopy(line(c, 2, half), h1.at[c, half], rs_send.at[c, 0], rs_recv.at[c, half], there(c, d, 0)).start()

    def reduce_2(c):
        for half, d in ((0, 1), (1, -1)):
            wait_bytes(h1.at[c, half], rs_recv.at[c, half])
            ref = line(c, d, half)
            ref[...] = plus(ref, h1.at[c, half]).astype(BF16)
            rcopy(line(c, d), f1.at[c, half], rs_send.at[c, 1], rs_recv.at[c, 2 + half], there(c, d, 0)).start()

    def reduce_3(c):
        for half in range(2):
            wait_bytes(f1.at[c, half], rs_recv.at[c, 2 + half])
        ref = line(c, 0)
        ref[...] = plus(ref, f1.at[c, 0], f1.at[c, 1]).astype(BF16)
        for half, e in ((0, 1), (1, -1)):
            rcopy(
                home(c, 2).at[half], h2.at[c, half], rs_send.at[c, 2], rs_recv.at[c, 4 + half], there(c, 0, e)
            ).start()

    def reduce_4(c):
        for half, e in ((0, 1), (1, -1)):
            wait_bytes(h2.at[c, half], rs_recv.at[c, 4 + half])
            ref = home(c, e).at[half]
            ref[...] = plus(ref, h2.at[c, half]).astype(BF16)
            rcopy(home(c, e), f2.at[c, half], rs_send.at[c, 3], rs_recv.at[c, 6 + half], there(c, 0, e)).start()

    def back(src, c, hi, lo, count):
        zz = jnp.int32(4 * hi + c)
        dst = ob.at[z, pl.ds(lo, count)]

        @pl.when(zz == z)
        def _():
            pltpu.make_async_copy(src, dst, ob_sem.at[1]).start()

        @pl.when(zz != z)
        def _():
            rcopy(src, dst, ob_sem.at[0], ob_sem.at[1], dev(x, y, zz, key)).start()

    def reduce_5(c):
        for half in range(2):
            wait_bytes(f2.at[c, half], rs_recv.at[c, 6 + half])
        ref = home(c, 0)
        for hi in range(2):
            for a in range(2):
                total = plus(ref.at[hi, a], f2.at[c, 0, hi, a], f2.at[c, 1, hi, a])
                fb[c, hi, a] = (total * FACTOR if a == 0 else total).astype(BF16)
            back(fb.at[c, hi], c, hi, 0, 2)

    def query_back(c):
        for hi in range(2):
            back(qb.at[c, pl.ds(hi, 1)], c, hi, 2, 1)

    def reduce_end(c):
        for i, ref in enumerate((h1, f1, h2, f2)):
            wait_bytes(ref.at[c], rs_send.at[c, i])

    bias_rows(0)
    for c in range(CHUNKS):
        gather_1(c)
    bias_rows(1)
    for c in range(CHUNKS):
        gather_2(c)
    bias_rows(2)
    for c in range(CHUNKS):
        gather_3(c)
    bias_rows(3)
    for c in range(CHUNKS):
        gather_4(c)

    wait_bytes(r_ref, qd_sem.at[1])
    wait_bytes(br, bias_sem.at[1])
    mask = jnp.where(ac_ref[...] > 0, 0.0, -jnp.inf).astype(F32)

    def widen(g, carry):
        at = pl.ds(pl.multiple_of(g * 16, 16), 16)
        bf[at] = (br[at].astype(F32) + mask[:, :LIVE]) * LOG2E
        return carry

    lax.fori_loop(0, 8, widen, 0)

    gather_5(0)
    attention(0)
    reduce_1(0)
    query_back(0)
    gather_5(1)
    attention(1)
    reduce_1(1)
    reduce_2(0)
    query_back(1)
    gather_5(2)
    attention(2)
    reduce_1(2)
    reduce_2(1)
    reduce_3(0)
    query_back(2)
    gather_5(3)
    attention(3)
    reduce_1(3)

    for hi in range(2):
        for col in range(7):
            dbs[hi * 8 + col] = db[hi * 64 : hi * 64 + 64, col * 256 : col * 256 + 256].astype(BF16)
    for dz, dk, zz, kk in zline():
        target = rem(zz, 4) * 2 + kk
        src = dbs.at[div(zz, 4) * 8 + target]
        dst = dr.at[head]

        @pl.when(target < 7)
        def _():
            if dz or dk:
                rcopy(src, dst, db_sem.at[0], db_sem.at[1], dev(x, y, zz, kk)).start()
            else:
                pltpu.make_async_copy(src, dst, db_sem.at[1]).start()

    query_back(3)
    reduce_2(2)
    reduce_3(1)
    reduce_4(0)
    reduce_2(3)
    reduce_3(2)
    reduce_4(1)
    reduce_5(0)
    reduce_3(3)
    reduce_4(2)
    reduce_5(1)
    reduce_4(3)
    reduce_5(2)

    @pl.when(live_cols)
    def _():
        wait_bytes(dr, db_sem.at[1])
        for h in range(16):
            wide = dr[h].astype(F32)
            for half in range(2):
                df[half, pl.ds(h * 64, 64)] = wide[:, half * 128 : half * 128 + 128]

        def step(r, acc):
            left = jnp.concatenate([df[half, pl.ds(r, 16, stride=64)] for half in range(2)], axis=1)
            return acc + dot(left.astype(BF16), n_ref[r])

        ra[y * 4 + x] = lax.fori_loop(0, 64, step, jnp.zeros((16, 128), F32))

    @pl.when(cidx == 7)
    def _():
        ra[y * 4 + x] = jnp.zeros((16, 128), F32)

    for dy in range(4):
        for dx in range(4):
            if dy or dx:
                mine = ra.at[y * 4 + x]
                rcopy(mine, mine, ar_sem.at[0], ar_sem.at[1], dev(rem(x + dx, 4), rem(y + dy, 4), z, key)).start()
    reduce_5(3)
    wait_bytes(ra.at[pl.ds(0, 15)], ar_sem.at[1])
    total = ra[0]
    for i in range(1, 16):
        total += ra[i]
    rb[head] = total
    for dz, dk, zz, kk in zline():
        if dz or dk:
            mine = rb.at[head]
            rcopy(mine, mine, ar_sem.at[2], ar_sem.at[3], dev(x, y, zz, kk)).start()

    wait_bytes(ob, ob_sem.at[1])
    for a in range(3):
        o_ref[a] = ob[:, a].reshape(8 * DH, 128).astype(F32).T.astype(BF16)

    wait_bytes(rb.at[pl.ds(0, 15)], ar_sem.at[3])
    summed = rb[0]
    for i in range(1, 16):
        summed += rb[i]
    wg_ref[...] = summed * gain_ref[...]
    gg_ref[...] = jnp.sum(summed * wt_ref[...], axis=0, keepdims=True)

    wait_bytes(skv.at[pl.ds(0, 7)], kv_send)
    wait_bytes(sqd.at[pl.ds(0, 7)], qd_sem.at[0])

    @pl.when(live_cols)
    def _():
        wait_bytes(bs.at[:, pl.ds(0, 15)], bias_sem.at[0])
        wait_bytes(dbs.at[pl.ds(0, 13)], db_sem.at[0])

    @pl.when(cidx == 7)
    def _():
        wait_bytes(dbs.at[pl.ds(0, 14)], db_sem.at[0])

    for c in range(CHUNKS):
        gather_end(c)
        reduce_end(c)
    wait_bytes(ob.at[pl.ds(0, 7)], ob_sem.at[0])
    wait_bytes(ra.at[pl.ds(0, 15)], ar_sem.at[0])
    wait_bytes(rb.at[pl.ds(0, 15)], ar_sem.at[2])


def fused(stacked, pair_feats, weight_t, gain, counts):
    vmem = pl.BlockSpec(memory_space=pltpu.VMEM)
    scratch = [
        pltpu.VMEM((64, 256, 128), BF16),
        pltpu.VMEM((8, 2, DH, 128), BF16),
        pltpu.VMEM((8, 2, DH, 128), BF16),
        pltpu.VMEM((4, 4, 4, 2, 2, DH, 128), BF16),
        pltpu.VMEM((4, 2, 2, DH, 128), BF16),
        pltpu.VMEM((2, 256, 128), F32),
        pltpu.VMEM((4, 16, 16, 256), BF16),
        pltpu.VMEM((ROWS, LIVE), BF16),
        pltpu.VMEM((ROWS, LIVE), F32),
        pltpu.VMEM((2, 2, DH, LIVE), BF16),
        pltpu.VMEM((2, 2, DH, 128), BF16),
        pltpu.VMEM((ROWS, LIVE), F32),
        pltpu.VMEM((ROWS, LIVE), F32),
        pltpu.VMEM((ROWS, LIVE), BF16),
        pltpu.VMEM((ROWS, LIVE), BF16),
        pltpu.VMEM((ROWS, LIVE), F32),
        pltpu.VMEM((2, 2, DH, LIVE), F32),
        pltpu.VMEM((2, DH, 128), F32),
        pltpu.VMEM((4, 4, 4, 2, 2, DH, 128), BF16),
        pltpu.VMEM((4, 2, DH, 128), BF16),
        pltpu.VMEM((4, 2, 4, 2, DH, 128), BF16),
        pltpu.VMEM((4, 2, 4, 2, 2, DH, 128), BF16),
        pltpu.VMEM((4, 2, 2, DH, 128), BF16),
        pltpu.VMEM((4, 2, 2, 2, DH, 128), BF16),
        pltpu.VMEM((4, 2, 2, DH, 128), BF16),
        pltpu.VMEM((8, 3, DH, 128), BF16),
        pltpu.VMEM((16, 64, 256), BF16),
        pltpu.VMEM((16, 64, 256), BF16),
        pltpu.VMEM((2, 1024, 128), F32),
        pltpu.VMEM((16, 16, 128), F32),
        pltpu.VMEM((16, 16, 128), F32),
        pltpu.SemaphoreType.DMA((4,)),
        pltpu.SemaphoreType.DMA,
        pltpu.SemaphoreType.DMA((4,)),
        pltpu.SemaphoreType.DMA((2,)),
        pltpu.SemaphoreType.DMA((2,)),
        pltpu.SemaphoreType.DMA((4, 4)),
        pltpu.SemaphoreType.DMA((4, 4, 4, 2)),
        pltpu.SemaphoreType.DMA((4, 4)),
        pltpu.SemaphoreType.DMA((4, 8)),
        pltpu.SemaphoreType.DMA((2,)),
        pltpu.SemaphoreType.DMA((2,)),
        pltpu.SemaphoreType.DMA((4,)),
    ]
    return pl.pallas_call(
        kernel,
        out_shape=(
            jax.ShapeDtypeStruct((3, 128, 8 * DH), BF16),
            jax.ShapeDtypeStruct((16, 128), F32),
            jax.ShapeDtypeStruct((1, 128), F32),
        ),
        in_specs=[vmem, pl.BlockSpec(memory_space=pl.ANY), vmem, vmem, vmem],
        out_specs=(vmem, vmem, vmem),
        scratch_shapes=scratch,
        compiler_params=pltpu.CompilerParams(
            collective_id=0, has_side_effects=True, vmem_limit_bytes=56 * 1024 * 1024
        ),
    )(stacked, pair_feats, weight_t, gain, counts)


def local(
    query_proj, key_proj, value_proj, grad_out, pair_feats, pair_gain, bias_weight, atom_counts
):
    stacked = jnp.stack([key_proj, value_proj, query_proj, grad_out])
    stacked = stacked.transpose(0, 2, 1, 3).reshape(4, 128, 8 * DH)
    out, weight_t, gain_grad = fused(
        stacked,
        pair_feats,
        bias_weight.astype(F32).T,
        pair_gain[None],
        atom_counts[None],
    )
    out = out.reshape(3, 2, 64, 8 * DH).transpose(0, 2, 1, 3)
    return out[2], out[0], out[1], weight_t.T, gain_grad[0]


def solution(mesh):
    tokens = P("qry", "smp", "key")
    return jax.shard_map(
        local,
        mesh=mesh,
        in_specs=(tokens, tokens, tokens, tokens, P("qry", ("smp", "key"), None), P(), P(), P()),
        out_specs=(tokens, tokens, tokens, P(), P()),
        check_vma=False,
    )
```

```python
import jax
import jax.numpy as jnp
from jax import lax
from jax.experimental import pallas as pl
from jax.experimental.pallas import tpu as pltpu
from jax.sharding import PartitionSpec as P

DH = 48
HEADS = 16
TOKENS = 2048
LIVE = 1792
ROWS = 128
CHUNKS = 4
PAIRS = 14
FACTOR = DH ** (-0.5)
LOG2E = 1.4426950408889634
MESH = pl.DeviceIdType.MESH
F32 = jnp.float32
BF16 = jnp.bfloat16


def rem(a, b):
    return lax.rem(a, jnp.int32(b))


def div(a, b):
    return lax.div(a, jnp.int32(b))


def dot(a, b):
    return jnp.dot(a, b, preferred_element_type=F32)


def dot_nt(a, b):
    return lax.dot_general(a, b, (((1,), (1,)), ((), ())), preferred_element_type=F32)


def wait_bytes(ref, sem):
    pltpu.make_async_copy(ref, ref, sem).wait()


def kernel(
    a_ref, x_ref, wt_ref, gain_ref, ac_ref,
    o_ref, wg_ref, gg_ref,
    n_ref, skv, sqd, g_ref, r_ref, bsf, bs, br, bf,
    kvt, qdt, s_ref, p_ref, w_ref, ds_ref, db, dkv, dq, d_ref, qb,
    h1, f1, h2, f2, fb, ob, dbs, dr, df, ra, rb,
    x_sem, kv_send, kv_recv, qd_sem, bias_sem, ag_send, ag_recv,
    rs_send, rs_recv, ob_sem, db_sem, ar_sem,
):
    smp = lax.axis_index("smp")
    qry = lax.axis_index("qry")
    key = lax.axis_index("key")
    y = div(qry, 8)
    zh = rem(div(qry, 4), 2)
    x = rem(qry, 4)
    z = zh * 4 + smp
    cidx = smp * 2 + key
    head = key * 8 + z
    live_cols = cidx < 7

    def dev(xx, yy, zz, kk):
        return (rem(zz, 4), yy * 8 + div(zz, 4) * 4 + xx, kk)

    def rcopy(src, dst, send, recv, device):
        return pltpu.make_async_remote_copy(
            src_ref=src, dst_ref=dst, send_sem=send, recv_sem=recv, device_id=device, device_id_type=MESH
        )

    def zline():
        for dz in range(8):
            for dk in range(2):
                yield dz, dk, rem(z + dz, 8), rem(key + dk, 2)

    x_copies = [
        pltpu.make_async_copy(x_ref.at[pl.ds(16 * rc, 16)], n_ref.at[pl.ds(16 * rc, 16)], x_sem.at[rc])
        for rc in range(4)
    ]
    for copy in x_copies:
        copy.start()

    barrier = pltpu.get_barrier_semaphore()
    for dz, dk, zz, kk in zline():
        if dz or dk:
            pl.semaphore_signal(barrier, inc=1, device_id=dev(x, y, zz, kk), device_id_type=MESH)
    for dy in range(4):
        for dx in range(4):
            if dy or dx:
                pl.semaphore_signal(
                    barrier, inc=1, device_id=dev(rem(x + dx, 4), rem(y + dy, 4), z, key), device_id_type=MESH
                )

    for a in range(4):
        turned = a_ref[a].astype(F32).T.astype(BF16).reshape(8, DH, 128)
        if a < 2:
            skv[:, a] = turned
        else:
            sqd[:, a - 2] = turned

    for c in range(CHUNKS):
        d_ref[c, 3, :, 1] = jnp.zeros((4, 2, DH, 128), BF16)

    gw = wt_ref[...].astype(F32) * gain_ref[...]
    gw_high = gw.astype(BF16)
    gw_low = (gw - gw_high.astype(F32)).astype(BF16)
    gw_both = jnp.concatenate([gw_high, gw_low], axis=0)
    mean_of = jnp.full((128, 128), 1.0 / 128, BF16)

    def bias_rows(rc):
        x_copies[rc].wait()

        def step(i, carry):
            row = rc * 16 + 2 * i
            tile = n_ref[pl.ds(row, 2)].reshape(512, 128)
            center = tile.astype(F32) - dot(tile, mean_of)
            square = center * center
            high = square.astype(BF16)
            low = (square - high.astype(F32)).astype(BF16)
            spread = dot(high, mean_of) + dot(low, mean_of)
            normed = (center * lax.rsqrt(spread + 1e-05)).astype(BF16)
            n_ref[pl.ds(row, 2)] = normed.reshape(2, 256, 128)
            out = dot_nt(gw_both, normed)
            out = out[:16] + out[16:]
            for j in range(2):
                for half in range(2):
                    bsf[half, pl.ds((2 * i + j) * 16, 16)] = out[:, j * 256 + half * 128 : j * 256 + half * 128 + 128]
            return carry

        lax.fori_loop(0, 8, step, 0, unroll=2)
        for h in range(16):
            pieces = [bsf[half, pl.ds(h, 16, stride=16)] for half in range(2)]
            bs[rc, h] = jnp.concatenate(pieces, axis=1).astype(BF16)

    def bias_send(rc):
        @pl.when(live_cols)
        def _():
            dst = br.at[pl.ds(zh * 64 + 16 * rc, 16), pl.ds(pl.multiple_of(cidx * 256, 256), 256)]
            for dz, dk, zz, kk in zline():
                src = bs.at[rc, kk * 8 + zz]
                if dz or dk:
                    rcopy(src, dst, bias_sem.at[0], bias_sem.at[1], dev(x, y, zz, kk)).start()
                else:
                    pltpu.make_async_copy(src, dst, bias_sem.at[1]).start()

    bias_rows(0)
    pl.semaphore_wait(barrier, 30)

    for dz in range(8):
        zz = rem(z + dz, 8)
        dst = g_ref.at[smp, y, x, zh]
        if dz == 0:
            pltpu.make_async_copy(skv.at[zz], dst, kv_recv.at[smp]).start()
        else:
            rcopy(skv.at[zz], dst, kv_send, kv_recv.at[smp], dev(x, y, zz, key)).start()
    for dz in range(8):
        zz = rem(z + dz, 8)
        dst = r_ref.at[smp, zh]
        if dz == 0:
            pltpu.make_async_copy(sqd.at[zz], dst, qd_sem.at[1]).start()
        else:
            rcopy(sqd.at[zz], dst, qd_sem.at[0], qd_sem.at[1], dev(x, y, zz, key)).start()

    bias_send(0)
    for rc in range(1, 4):
        bias_rows(rc)
        bias_send(rc)

    def spot(c, dp, dq):
        dx, dy = (dp, dq) if c % 2 == 0 else (dq, dp)
        return rem(x + dx + 4, 4), rem(y + dy + 4, 4)

    def there(c, dp, dq):
        xx, yy = spot(c, dp, dq)
        return dev(xx, yy, z, key)

    def block(c, dp, dq):
        xx, yy = spot(c, dp, dq)
        return (c, yy, xx)

    def gather_send(c, where, half, sem, target):
        src = g_ref.at[where] if half is None else g_ref.at[where + (half,)]
        rcopy(src, src, ag_send.at[c, sem], ag_recv.at[where + (half or 0,)], target).start()

    def gather_wait(where, half):
        ref = g_ref.at[where] if half is None else g_ref.at[where + (half,)]
        wait_bytes(ref, ag_recv.at[where + (half or 0,)])

    def gather_1(c):
        wait_bytes(g_ref.at[c, y, x], kv_recv.at[c])
        for dp in (1, -1, 2):
            gather_send(c, block(c, 0, 0), None, 0, there(c, dp, 0))

    def gather_2(c, steps):
        for dp in (0, 1, -1, 2):
            where = block(c, dp, 0)
            if dp:
                gather_wait(where, None)
            for dq in steps:
                gather_send(c, where, None, 1, there(c, 0, dq))

    def gather_3(c):
        for dp in (0, 1, -1, 2):
            for half, dq in ((0, 1), (1, -1)):
                where = block(c, dp, -dq)
                gather_wait(where, None)
                gather_send(c, where, half, 2, there(c, 0, dq))

    def gather_4(c):
        for dp in (0, 1, -1, 2):
            if c < 2:
                for half in range(2):
                    gather_wait(block(c, dp, 2), half)
            else:
                for dq in (1, -1, 2):
                    gather_wait(block(c, dp, dq), None)

    def gather_end(c):
        wait_bytes(g_ref.at[c, 0, pl.ds(0, 3)], ag_send.at[c, 0])
        if c < 2:
            wait_bytes(g_ref.at[c, pl.ds(0, 2)], ag_send.at[c, 1])
            wait_bytes(g_ref.at[c, 0], ag_send.at[c, 2])
        else:
            wait_bytes(g_ref.at[c, pl.ds(0, 3)], ag_send.at[c, 1])

    low_lanes = lax.broadcasted_iota(jnp.int32, (DH, 128), 1) < 64

    def merge(first, second):
        return (
            jnp.where(low_lanes, first, pltpu.roll(second, 64, 1)),
            jnp.where(low_lanes, pltpu.roll(first, 64, 1), second),
        )

    def tiles():
        for yy in range(4):
            for hi in range(2):
                for m in range(2):
                    if yy < 3 or hi == 0:
                        yield yy, hi, m, slice((yy * 4 + hi * 2 + m) * 128, (yy * 4 + hi * 2 + m + 1) * 128)

    def spread(c):
        for yy, hi, m, lanes in tiles():
            for a in range(2):
                both = merge(g_ref[c, yy, 2 * m, hi, a].astype(F32), g_ref[c, yy, 2 * m + 1, hi, a].astype(F32))
                for par in range(2):
                    kvt[2 * c + par, a, :, lanes] = both[par].astype(BF16)
        for a in range(2):
            both = merge(r_ref[c, 0, a].astype(F32), r_ref[c, 1, a].astype(F32))
            for par in range(2):
                qdt[2 * c + par, a] = both[par].astype(BF16)

    def scores_of(s):
        turned = [qdt[s, a].astype(F32).T.astype(BF16) for a in range(2)]
        s_ref[s % 2] = dot(turned[0], kvt[s, 0])
        p_ref[s % 2] = dot(turned[1], kvt[s, 1])

    def softmax_of(s):
        for g in range(8):
            at = slice(g * 16, g * 16 + 16)
            scores = s_ref[s % 2, at] * (FACTOR * LOG2E) + bf[at]
            top = jnp.max(scores, axis=1, keepdims=True)
            exponent = jnp.exp2(scores - top)
            slopes = p_ref[s % 2, at]
            total = jnp.sum(exponent, axis=1, keepdims=True)
            mixed = jnp.sum(exponent * slopes, axis=1, keepdims=True)
            inverse = 1.0 / total
            weights = exponent * inverse
            score_grad = weights * (slopes - mixed * inverse)
            w_ref[s % 4, at] = weights.astype(BF16)
            ds_ref[s % 4, at] = score_grad.astype(BF16)
            if s:
                db[at] += score_grad
            else:
                db[at] = score_grad

    def grads_of(s):
        dkv[s % 2, 0] = dot(qdt[s, 0], ds_ref[s % 4])
        dkv[s % 2, 1] = dot(qdt[s, 1], w_ref[s % 4])
        dq[s % 2] = dot_nt(kvt[s, 0], ds_ref[s % 4]) * FACTOR

    def collect(c):
        for yy, hi, m, lanes in tiles():
            for a in range(2):
                both = merge(dkv[0, a, :, lanes], dkv[1, a, :, lanes])
                for e in range(2):
                    d_ref[c, yy, 2 * m + e, hi, a] = both[e].astype(BF16)
        both = merge(dq[0], dq[1])
        for hi in range(2):
            qb[c, hi] = both[hi].astype(BF16)

    def line(c, dp, half=None):
        xx, yy = spot(c, dp, 0)
        ref = d_ref.at[c, :, xx] if c % 2 == 0 else d_ref.at[c, yy]
        return ref if half is None else ref.at[:, half]

    def home(c, dq):
        return d_ref.at[block(c, 0, dq)]

    def plus(ref, *others):
        total = ref[...].astype(F32)
        for other in others:
            total += other[...].astype(F32)
        return total

    def reduce_1(c):
        for half, d in ((0, 1), (1, -1)):
            rcopy(line(c, 2, half), h1.at[c, half], rs_send.at[c, 0], rs_recv.at[c, half], there(c, d, 0)).start()

    def reduce_2(c):
        for half, d in ((0, 1), (1, -1)):
            wait_bytes(h1.at[c, half], rs_recv.at[c, half])
            ref = line(c, d, half)
            ref[...] = plus(ref, h1.at[c, half]).astype(BF16)
            rcopy(line(c, d), f1.at[c, half], rs_send.at[c, 1], rs_recv.at[c, 2 + half], there(c, d, 0)).start()

    def reduce_3(c):
        for half in range(2):
            wait_bytes(f1.at[c, half], rs_recv.at[c, 2 + half])
        ref = line(c, 0)
        ref[...] = plus(ref, f1.at[c, 0], f1.at[c, 1]).astype(BF16)
        for half, e in ((0, 1), (1, -1)):
            rcopy(
                home(c, 2).at[half], h2.at[c, half], rs_send.at[c, 2], rs_recv.at[c, 4 + half], there(c, 0, e)
            ).start()

    def reduce_4(c):
        for half, e in ((0, 1), (1, -1)):
            wait_bytes(h2.at[c, half], rs_recv.at[c, 4 + half])
            ref = home(c, e).at[half]
            ref[...] = plus(ref, h2.at[c, half]).astype(BF16)
            rcopy(home(c, e), f2.at[c, half], rs_send.at[c, 3], rs_recv.at[c, 6 + half], there(c, 0, e)).start()

    def back(src, c, hi, lo, count):
        zz = jnp.int32(4 * hi + c)
        dst = ob.at[z, pl.ds(lo, count)]

        @pl.when(zz == z)
        def _():
            pltpu.make_async_copy(src, dst, ob_sem.at[1]).start()

        @pl.when(zz != z)
        def _():
            rcopy(src, dst, ob_sem.at[0], ob_sem.at[1], dev(x, y, zz, key)).start()

    def reduce_5(c):
        for half in range(2):
            wait_bytes(f2.at[c, half], rs_recv.at[c, 6 + half])
        ref = home(c, 0)
        for hi in range(2):
            for a in range(2):
                total = plus(ref.at[hi, a], f2.at[c, 0, hi, a], f2.at[c, 1, hi, a])
                fb[c, hi, a] = (total * FACTOR if a == 0 else total).astype(BF16)
            back(fb.at[c, hi], c, hi, 0, 2)

    def query_back(c):
        for hi in range(2):
            back(qb.at[c, pl.ds(hi, 1)], c, hi, 2, 1)

    def reduce_end(c):
        for i, ref in enumerate((h1, f1, h2, f2)):
            wait_bytes(ref.at[c], rs_send.at[c, i])

    for c in range(CHUNKS):
        gather_1(c)
    for c in range(2):
        gather_2(c, (1, -1))
    for c in range(2):
        gather_3(c)
    for c in range(2, 4):
        gather_2(c, (1, -1, 2))

    wait_bytes(r_ref, qd_sem.at[1])
    wait_bytes(br, bias_sem.at[1])
    mask = jnp.where(ac_ref[...] > 0, 0.0, -jnp.inf).astype(F32)
    for g in range(8):
        at = slice(g * 16, g * 16 + 16)
        bf[at] = (br[at].astype(F32) + mask[:, :LIVE]) * LOG2E

    for c in range(2):
        gather_4(c)
        spread(c)
        scores_of(2 * c)
        scores_of(2 * c + 1)
        softmax_of(2 * c)
        grads_of(2 * c)
        softmax_of(2 * c + 1)
        grads_of(2 * c + 1)
        collect(c)
        reduce_1(c)
        query_back(c)

    for c in range(2, 4):
        gather_4(c)
        spread(c)
        scores_of(2 * c)
        scores_of(2 * c + 1)
        softmax_of(2 * c)
        softmax_of(2 * c + 1)

    for hi in range(2):
        for col in range(7):
            dbs[hi * 8 + col] = db[hi * 64 : hi * 64 + 64, col * 256 : col * 256 + 256].astype(BF16)
    for dz, dk, zz, kk in zline():
        target = rem(zz, 4) * 2 + kk
        src = dbs.at[div(zz, 4) * 8 + target]
        dst = dr.at[head]

        @pl.when(target < 7)
        def _():
            if dz or dk:
                rcopy(src, dst, db_sem.at[0], db_sem.at[1], dev(x, y, zz, kk)).start()
            else:
                pltpu.make_async_copy(src, dst, db_sem.at[1]).start()

    reduce_2(0)
    grads_of(4)
    grads_of(5)
    collect(2)
    reduce_1(2)
    reduce_2(1)
    query_back(2)
    grads_of(6)
    grads_of(7)
    collect(3)
    reduce_1(3)
    query_back(3)
    reduce_3(0)
    reduce_3(1)
    reduce_2(2)
    reduce_4(0)
    reduce_2(3)
    reduce_4(1)
    reduce_5(0)
    reduce_5(1)
    reduce_3(2)
    reduce_3(3)

    @pl.when(live_cols)
    def _():
        wait_bytes(dr, db_sem.at[1])
        for h in range(16):
            wide = dr[h].astype(F32)
            for half in range(2):
                df[half, pl.ds(h * 64, 64)] = wide[:, half * 128 : half * 128 + 128]

        def step(r, acc):
            left = jnp.concatenate([df[half, pl.ds(r, 16, stride=64)] for half in range(2)], axis=1)
            return acc + dot(left.astype(BF16), n_ref[r])

        ra[y * 4 + x] = lax.fori_loop(0, 64, step, jnp.zeros((16, 128), F32), unroll=8)

    @pl.when(cidx == 7)
    def _():
        ra[y * 4 + x] = jnp.zeros((16, 128), F32)

    for dy in range(4):
        for dx in range(4):
            if dy or dx:
                mine = ra.at[y * 4 + x]
                rcopy(mine, mine, ar_sem.at[0], ar_sem.at[1], dev(rem(x + dx, 4), rem(y + dy, 4), z, key)).start()
    reduce_4(2)
    reduce_4(3)
    wait_bytes(ra.at[pl.ds(0, 15)], ar_sem.at[1])
    total = ra[0]
    for i in range(1, 16):
        total += ra[i]
    rb[head] = total
    for dz, dk, zz, kk in zline():
        if dz or dk:
            mine = rb.at[head]
            rcopy(mine, mine, ar_sem.at[2], ar_sem.at[3], dev(x, y, zz, kk)).start()

    reduce_5(2)
    reduce_5(3)
    wait_bytes(ob, ob_sem.at[1])
    for a in range(3):
        o_ref[a] = ob[:, a].reshape(8 * DH, 128).astype(F32).T.astype(BF16)

    wait_bytes(rb.at[pl.ds(0, 15)], ar_sem.at[3])
    summed = rb[0]
    for i in range(1, 16):
        summed += rb[i]
    wg_ref[...] = summed * gain_ref[...]
    gg_ref[...] = jnp.sum(summed * wt_ref[...].astype(F32), axis=0, keepdims=True)

    wait_bytes(skv.at[pl.ds(0, 7)], kv_send)
    wait_bytes(sqd.at[pl.ds(0, 7)], qd_sem.at[0])

    @pl.when(live_cols)
    def _():
        wait_bytes(bs.at[:, pl.ds(0, 15)], bias_sem.at[0])
        wait_bytes(dbs.at[pl.ds(0, 13)], db_sem.at[0])

    @pl.when(cidx == 7)
    def _():
        wait_bytes(dbs.at[pl.ds(0, 14)], db_sem.at[0])

    for c in range(CHUNKS):
        gather_end(c)
        reduce_end(c)
    wait_bytes(ob.at[pl.ds(0, 7)], ob_sem.at[0])
    wait_bytes(ra.at[pl.ds(0, 15)], ar_sem.at[0])
    wait_bytes(rb.at[pl.ds(0, 15)], ar_sem.at[2])


def fused(stacked, pair_feats, weight_t, gain, counts):
    vmem = pl.BlockSpec(memory_space=pltpu.VMEM)
    scratch = [
        pltpu.VMEM((64, 256, 128), BF16),
        pltpu.VMEM((8, 2, DH, 128), BF16),
        pltpu.VMEM((8, 2, DH, 128), BF16),
        pltpu.VMEM((4, 4, 4, 2, 2, DH, 128), BF16),
        pltpu.VMEM((4, 2, 2, DH, 128), BF16),
        pltpu.VMEM((2, 256, 128), F32),
        pltpu.VMEM((4, 16, 16, 256), BF16),
        pltpu.VMEM((ROWS, LIVE), BF16),
        pltpu.VMEM((ROWS, LIVE), F32),
        pltpu.VMEM((8, 2, DH, LIVE), BF16),
        pltpu.VMEM((8, 2, DH, 128), BF16),
        pltpu.VMEM((2, ROWS, LIVE), F32),
        pltpu.VMEM((2, ROWS, LIVE), F32),
        pltpu.VMEM((4, ROWS, LIVE), BF16),
        pltpu.VMEM((4, ROWS, LIVE), BF16),
        pltpu.VMEM((ROWS, LIVE), F32),
        pltpu.VMEM((2, 2, DH, LIVE), F32),
        pltpu.VMEM((2, DH, 128), F32),
        pltpu.VMEM((4, 4, 4, 2, 2, DH, 128), BF16),
        pltpu.VMEM((4, 2, DH, 128), BF16),
        pltpu.VMEM((4, 2, 4, 2, DH, 128), BF16),
        pltpu.VMEM((4, 2, 4, 2, 2, DH, 128), BF16),
        pltpu.VMEM((4, 2, 2, DH, 128), BF16),
        pltpu.VMEM((4, 2, 2, 2, DH, 128), BF16),
        pltpu.VMEM((4, 2, 2, DH, 128), BF16),
        pltpu.VMEM((8, 3, DH, 128), BF16),
        pltpu.VMEM((16, 64, 256), BF16),
        pltpu.VMEM((16, 64, 256), BF16),
        pltpu.VMEM((2, 1024, 128), F32),
        pltpu.VMEM((16, 16, 128), F32),
        pltpu.VMEM((16, 16, 128), F32),
        pltpu.SemaphoreType.DMA((4,)),
        pltpu.SemaphoreType.DMA,
        pltpu.SemaphoreType.DMA((4,)),
        pltpu.SemaphoreType.DMA((2,)),
        pltpu.SemaphoreType.DMA((2,)),
        pltpu.SemaphoreType.DMA((4, 3)),
        pltpu.SemaphoreType.DMA((4, 4, 4, 2)),
        pltpu.SemaphoreType.DMA((4, 4)),
        pltpu.SemaphoreType.DMA((4, 8)),
        pltpu.SemaphoreType.DMA((2,)),
        pltpu.SemaphoreType.DMA((2,)),
        pltpu.SemaphoreType.DMA((4,)),
    ]
    return pl.pallas_call(
        kernel,
        out_shape=(
            jax.ShapeDtypeStruct((3, 128, 8 * DH), BF16),
            jax.ShapeDtypeStruct((16, 128), F32),
            jax.ShapeDtypeStruct((1, 128), F32),
        ),
        in_specs=[vmem, pl.BlockSpec(memory_space=pl.ANY), vmem, vmem, vmem],
        out_specs=(vmem, vmem, vmem),
        scratch_shapes=scratch,
        compiler_params=pltpu.CompilerParams(
            collective_id=0, has_side_effects=True, vmem_limit_bytes=56 * 1024 * 1024
        ),
    )(stacked, pair_feats, weight_t, gain, counts)


def local(
    query_proj, key_proj, value_proj, grad_out, pair_feats, pair_gain, bias_weight, atom_counts
):
    stacked = jnp.stack([key_proj, value_proj, query_proj, grad_out])
    stacked = stacked.transpose(0, 2, 1, 3).reshape(4, 128, 8 * DH)
    out, weight_t, gain_grad = fused(
        stacked,
        pair_feats,
        bias_weight.T,
        pair_gain[None],
        atom_counts[None],
    )
    out = out.reshape(3, 2, 64, 8 * DH).transpose(0, 2, 1, 3)
    return out[2], out[0], out[1], weight_t.T, gain_grad[0]


def solution(mesh):
    tokens = P("qry", "smp", "key")
    return jax.shard_map(
        local,
        mesh=mesh,
        in_specs=(tokens, tokens, tokens, tokens, P("qry", ("smp", "key"), None), P(), P(), P()),
        out_specs=(tokens, tokens, tokens, P(), P()),
        check_vma=False,
    )
```

```python
import jax
import jax.numpy as jnp
from jax import lax
from jax.experimental import pallas as pl
from jax.experimental.pallas import tpu as pltpu
from jax.sharding import PartitionSpec as P

DH = 48
HEADS = 16
TOKENS = 2048
LIVE = 1792
ROWS = 128
CHUNKS = 4
PAIRS = 14
FACTOR = DH ** (-0.5)
LOG2E = 1.4426950408889634
MESH = pl.DeviceIdType.MESH
F32 = jnp.float32
BF16 = jnp.bfloat16


def rem(a, b):
    return lax.rem(a, jnp.int32(b))


def div(a, b):
    return lax.div(a, jnp.int32(b))


def dot(a, b):
    return jnp.dot(a, b, preferred_element_type=F32)


def dot_nt(a, b):
    return lax.dot_general(a, b, (((1,), (1,)), ((), ())), preferred_element_type=F32)


def wait_bytes(ref, sem):
    pltpu.make_async_copy(ref, ref, sem).wait()


def kernel(
    ak_ref, av_ref, aq_ref, ag_ref, x_ref, wt_ref, gain_ref, ac_ref,
    o_ref, sum_ref,
    n_ref, skv, sqd, g_ref, r_ref, bsf, bs, br, bf,
    kvt, qdt, s_ref, p_ref, w_ref, ds_ref, db, dkv, dq, d_ref, qb,
    e_ref, f_ref, h_ref, fb, ob, dbs, dr, df, ra, rb,
    x_sem, kv_send, kv_recv, qd_sem, bias_sem, ag_send, ag_recv,
    rs_send, rs_recv, ob_sem, db_sem, ar_sem,
):
    smp = lax.axis_index("smp")
    qry = lax.axis_index("qry")
    key = lax.axis_index("key")
    y = div(qry, 8)
    zh = rem(div(qry, 4), 2)
    x = rem(qry, 4)
    z = zh * 4 + smp
    cidx = smp * 2 + key
    lx = rem(x, 2)
    vx = x - lx + key
    vx2 = rem(vx + 2, 4)
    sx = x - lx + 1 - key
    sx2 = rem(sx + 2, 4)
    head = lx * 8 + z
    same = key == lx
    live_cols = cidx < 7

    def dev(xx, yy, zz, kk):
        return (rem(zz, 4), yy * 8 + div(zz, 4) * 4 + xx, kk)

    def rcopy(src, dst, send, recv, device):
        return pltpu.make_async_remote_copy(
            src_ref=src, dst_ref=dst, send_sem=send, recv_sem=recv, device_id=device, device_id_type=MESH
        )

    def owner(zz, half):
        return dev(x - lx + half, y, zz, lx)

    def source(zz, kk):
        return dev(vx, y, zz, kk)

    def there(dx, dy):
        return dev(rem(x + dx, 4), rem(y + dy, 4), z, key)

    sibling = dev(x, y, z, 1 - key)

    def send(src, dst, sems, device, first):
        if not first:
            rcopy(src, dst, sems[0], sems[1], device).start()
            return

        @pl.when(same)
        def _():
            pltpu.make_async_copy(src, dst, sems[1]).start()

        @pl.when(jnp.logical_not(same))
        def _():
            rcopy(src, dst, sems[0], sems[1], device).start()

    x_copies = [
        pltpu.make_async_copy(x_ref.at[pl.ds(16 * rc, 16)], n_ref.at[pl.ds(16 * rc, 16)], x_sem.at[rc])
        for rc in range(4)
    ]
    for copy in x_copies:
        copy.start()

    barrier = pltpu.get_barrier_semaphore()
    near = []
    for dz in range(8):
        for dx in range(2):
            for dk in range(2):
                if dz or dx or dk:
                    near.append(dev(x - lx + rem(lx + dx, 2), y, rem(z + dz, 8), rem(key + dk, 2)))
    for dy in range(4):
        for dx in range(4):
            if dy or dx == 2:
                near.append(there(dx, dy))
    near.append(dev(rem(x + 3 - 2 * lx, 4), y, z, key))
    for device in near:
        pl.semaphore_signal(barrier, inc=1, device_id=device, device_id_type=MESH)

    a_refs = (ak_ref, av_ref, aq_ref, ag_ref)

    def turned(a):
        whole = a_refs[a][...].astype(F32)
        return jnp.concatenate([whole[:, i] for i in range(2)], axis=0).T.astype(BF16).reshape(8, DH, 128)

    for a in range(2):
        skv[:, a] = turned(a)

    gw = wt_ref[...].astype(F32) * gain_ref[...]
    gw_high = gw.astype(BF16)
    gw_low = (gw - gw_high.astype(F32)).astype(BF16)
    gw_both = jnp.concatenate([gw_high, gw_low], axis=0)

    def bias_rows(rc):
        x_copies[rc].wait()

        def step(i, carry):
            row = rc * 16 + 2 * i
            tile = n_ref[pl.ds(row, 2)].reshape(512, 128)
            wide = tile.astype(F32)
            center = wide - jnp.mean(wide, axis=1, keepdims=True)
            spread = jnp.mean(center * center, axis=1, keepdims=True)
            normed = (center * lax.rsqrt(spread + 1e-05)).astype(BF16)
            n_ref[pl.ds(row, 2)] = normed.reshape(2, 256, 128)
            out = dot_nt(gw_both, normed)
            out = out[:16] + out[16:]
            for j in range(2):
                for half in range(2):
                    bsf[half, pl.ds((2 * i + j) * 16, 16)] = out[:, j * 256 + half * 128 : j * 256 + half * 128 + 128]
            return carry

        lax.fori_loop(0, 8, step, 0, unroll=4)
        for h in range(16):
            pieces = [bsf[half, pl.ds(h, 16, stride=16)] for half in range(2)]
            bs[rc, h] = jnp.concatenate(pieces, axis=1).astype(BF16)

    def bias_send(rc):
        @pl.when(live_cols)
        def _():
            dst = br.at[pl.ds(zh * 64 + 16 * rc, 16), pl.ds(pl.multiple_of(cidx * 256, 256), 256)]
            for dz in range(8):
                for dk in range(2):
                    zz, half = rem(z + dz, 8), rem(lx + dk, 2)
                    src = bs.at[rc, half * 8 + zz]
                    send(src, dst, (bias_sem.at[0], bias_sem.at[1]), owner(zz, half), dz + dk == 0)

    bias_rows(0)
    pl.semaphore_wait(barrier, len(near))

    for dz in range(8):
        zz = rem(z + dz, 8)
        send(skv.at[zz], g_ref.at[smp, y, x, zh], (kv_send, kv_recv.at[smp]), owner(zz, key), dz == 0)

    bias_send(0)
    for c in range(CHUNKS):
        d_ref[c, 3, :, 1] = jnp.zeros((4, 2, DH, 128), BF16)
    bias_rows(1)
    bias_send(1)

    def gather_send(c, yy, xx, device):
        ref = g_ref.at[c, yy, xx]
        rcopy(ref, ref, ag_send.at[c], ag_recv.at[c, yy, xx], device).start()

    def gather_wait(c, yy, xx):
        wait_bytes(g_ref.at[c, yy, xx], ag_recv.at[c, yy, xx])

    lines = [rem(y + dy, 4) for dy in range(4)]

    def gather_1(c):
        wait_bytes(g_ref.at[c, y, vx], kv_recv.at[c])
        gather_send(c, y, vx, there(2, 0))
        for dy in (1, 3, 2):
            gather_send(c, y, vx, there(0, dy))
        gather_send(c, y, vx, sibling)

    def gather_2(c):
        if c % 2 == 0:
            gather_wait(c, y, vx2)
            for dy in (1, 3, 2):
                gather_send(c, y, vx2, there(0, dy))
            gather_send(c, y, vx2, sibling)
        else:
            for dy in (1, 3, 2):
                gather_wait(c, lines[dy], vx)
                gather_send(c, lines[dy], vx, there(2, 0))
                gather_send(c, lines[dy], vx, sibling)

    def gather_3(c):
        if c % 2 == 0:
            for dy in (1, 3, 2):
                for xx in (vx, vx2):
                    gather_wait(c, lines[dy], xx)
                    gather_send(c, lines[dy], xx, sibling)
        else:
            for dy in (0, 1, 3, 2):
                gather_wait(c, lines[dy], vx2)
                gather_send(c, lines[dy], vx2, sibling)

    def gather_4(c):
        for yy in range(4):
            for xx in (sx, sx2):
                gather_wait(c, yy, xx)

    low_lanes = lax.broadcasted_iota(jnp.int32, (DH, 128), 1) < 64

    def merge(first, second):
        return (
            jnp.where(low_lanes, first, pltpu.roll(second, 64, 1)),
            jnp.where(low_lanes, pltpu.roll(first, 64, 1), second),
        )

    def tiles():
        for yy in range(4):
            for hi in range(2):
                for m in range(2):
                    if yy < 3 or hi == 0:
                        yield yy, hi, m, slice((yy * 4 + hi * 2 + m) * 128, (yy * 4 + hi * 2 + m + 1) * 128)

    def spread(c):
        for yy, hi, m, lanes in tiles():
            for a in range(2):
                both = merge(g_ref[c, yy, 2 * m, hi, a].astype(F32), g_ref[c, yy, 2 * m + 1, hi, a].astype(F32))
                for par in range(2):
                    kvt[2 * c + par, a, :, lanes] = both[par].astype(BF16)
        for a in range(2):
            both = merge(r_ref[c, 0, a].astype(F32), r_ref[c, 1, a].astype(F32))
            for par in range(2):
                qdt[2 * c + par, a] = both[par].astype(BF16)

    def scores_of(s):
        turned = [qdt[s, a].astype(F32).T.astype(BF16) for a in range(2)]
        s_ref[s % 2] = dot(turned[0], kvt[s, 0])
        p_ref[s % 2] = dot(turned[1], kvt[s, 1])

    def softmax_of(s):
        for g in range(8):
            at = slice(g * 16, g * 16 + 16)
            scores = s_ref[s % 2, at] * (FACTOR * LOG2E) + bf[at]
            top = jnp.max(scores, axis=1, keepdims=True)
            exponent = jnp.exp2(scores - top)
            slopes = p_ref[s % 2, at]
            total = jnp.sum(exponent, axis=1, keepdims=True)
            mixed = jnp.sum(exponent * slopes, axis=1, keepdims=True)
            inverse = 1.0 / total
            weights = exponent * inverse
            score_grad = weights * (slopes - mixed * inverse)
            w_ref[s % 4, at] = weights.astype(BF16)
            ds_ref[s % 4, at] = score_grad.astype(BF16)
            if s:
                db[at] += score_grad
            else:
                db[at] = score_grad

    def grads_of(s):
        dkv[s % 2, 0] = dot(qdt[s, 0], ds_ref[s % 4])
        dkv[s % 2, 1] = dot(qdt[s, 1], w_ref[s % 4])
        dq[s % 2] = dot_nt(kvt[s, 0], ds_ref[s % 4]) * FACTOR

    def collect(c):
        for yy, hi, m, lanes in tiles():
            for a in range(2):
                both = merge(dkv[0, a, :, lanes], dkv[1, a, :, lanes])
                for e in range(2):
                    d_ref[c, yy, 2 * m + e, hi, a] = both[e].astype(BF16)
        both = merge(dq[0], dq[1])
        for hi in range(2):
            qb[c, hi] = both[hi].astype(BF16)

    def plus(ref, *others):
        total = ref[...].astype(F32)
        for other in others:
            total += other[...].astype(F32)
        return total

    def reduce_1(c):
        for j, xx in enumerate((sx, sx2)):
            rcopy(d_ref.at[c, :, xx], e_ref.at[c, j], rs_send.at[c, 0], rs_recv.at[c, 0], sibling).start()

    def reduce_2(c):
        wait_bytes(e_ref.at[c], rs_recv.at[c, 0])
        for j, xx in ((1, vx2), (0, vx)):
            for yy in range(4):
                ref = d_ref.at[c, yy, xx]
                ref[...] = plus(ref, e_ref.at[c, j, yy]).astype(BF16)
            if c % 2 and j:
                rcopy(d_ref.at[c, :, vx2], h_ref.at[c], rs_send.at[c, 1], rs_recv.at[c, 1], there(2, 0)).start()
        if c % 2 == 0:
            for dy in (2, 1, 3):
                for j, xx in enumerate((vx, vx2)):
                    rcopy(
                        d_ref.at[c, lines[dy], xx], f_ref.at[c, j, dy - 1],
                        rs_send.at[c, 1], rs_recv.at[c, 1], there(0, dy),
                    ).start()

    def reduce_3(c):
        if c % 2 == 0:
            wait_bytes(f_ref.at[c], rs_recv.at[c, 1])
            for j, xx in ((1, vx2), (0, vx)):
                ref = d_ref.at[c, y, xx]
                ref[...] = plus(ref, *(f_ref.at[c, j, i] for i in range(3))).astype(BF16)
                if j:
                    rcopy(ref, h_ref.at[c, 0], rs_send.at[c, 2], rs_recv.at[c, 2], there(2, 0)).start()
        else:
            wait_bytes(h_ref.at[c], rs_recv.at[c, 1])
            for dy in (2, 1, 3, 0):
                ref = d_ref.at[c, lines[dy], vx]
                ref[...] = plus(ref, h_ref.at[c, lines[dy]]).astype(BF16)
                if dy:
                    rcopy(
                        ref, f_ref.at[c, 0, dy - 1], rs_send.at[c, 2], rs_recv.at[c, 2], there(0, dy)
                    ).start()

    def reduce_4(c):
        if c % 2 == 0:
            wait_bytes(h_ref.at[c, 0], rs_recv.at[c, 2])
            others = [h_ref.at[c, 0]]
        else:
            wait_bytes(f_ref.at[c, 0], rs_recv.at[c, 2])
            others = [f_ref.at[c, 0, i] for i in range(3)]
        for hi in range(2):
            for a in range(2):
                total = plus(d_ref.at[c, y, vx, hi, a], *(other.at[hi, a] for other in others))
                fb[c, hi, a] = (total * FACTOR if a == 0 else total).astype(BF16)
            back(fb.at[c, hi], c, hi, 0, 2)

    def back(src, c, hi, lo, count):
        zz = jnp.int32(4 * hi + c)
        dst = ob.at[z, pl.ds(lo, count)]
        here = jnp.logical_and(same, zz == z)

        @pl.when(here)
        def _():
            pltpu.make_async_copy(src, dst, ob_sem.at[1]).start()

        @pl.when(jnp.logical_not(here))
        def _():
            rcopy(src, dst, ob_sem.at[0], ob_sem.at[1], source(zz, lx)).start()

    def query_back(c):
        for hi in range(2):
            back(qb.at[c, pl.ds(hi, 1)], c, hi, 2, 1)

    def reduce_end(c):
        sizes = (8, 6, 1) if c % 2 == 0 else (8, 4, 3)
        for i, size in enumerate(sizes):
            wait_bytes(blocks(size), rs_send.at[c, i])

    def blocks(count):
        return n_ref.at[pl.ds(0, 3 * count), pl.ds(0, 64)]

    for c in range(CHUNKS):
        gather_1(c)
    for a in range(2):
        sqd[:, a] = turned(2 + a)
    for dz in range(8):
        zz = rem(z + dz, 8)
        send(sqd.at[zz], r_ref.at[smp, zh], (qd_sem.at[0], qd_sem.at[1]), owner(zz, key), dz == 0)
    bias_rows(2)
    bias_send(2)
    for c in range(2):
        gather_2(c)
    bias_rows(3)
    bias_send(3)
    for c in range(2, CHUNKS):
        gather_2(c)
    for c in range(2):
        gather_3(c)

    wait_bytes(r_ref, qd_sem.at[1])
    wait_bytes(br, bias_sem.at[1])
    mask = jnp.where(ac_ref[...] > 0, 0.0, -jnp.inf).astype(F32)
    for g in range(8):
        at = slice(g * 16, g * 16 + 16)
        bf[at] = (br[at].astype(F32) + mask[:, :LIVE]) * LOG2E

    for c in range(2):
        gather_4(c)
        spread(c)
        scores_of(2 * c)
        scores_of(2 * c + 1)
        softmax_of(2 * c)
        grads_of(2 * c)
        softmax_of(2 * c + 1)
        grads_of(2 * c + 1)
        collect(c)
        reduce_1(c)
        query_back(c)
        gather_3(c + 2)

    for c in range(2, 4):
        gather_4(c)
        spread(c)
        scores_of(2 * c)
        scores_of(2 * c + 1)
        reduce_2(c - 2)
        softmax_of(2 * c)
        softmax_of(2 * c + 1)

    for hi in range(2):
        for col in range(7):
            dbs[hi * 8 + col] = db[hi * 64 : hi * 64 + 64, col * 256 : col * 256 + 256].astype(BF16)
    for dz in range(8):
        for dk in range(2):
            zz, kk = rem(z + dz, 8), rem(key + dk, 2)
            target = rem(zz, 4) * 2 + kk
            src = dbs.at[div(zz, 4) * 8 + target]

            @pl.when(target < 7)
            def _():
                send(src, dr.at[head], (db_sem.at[0], db_sem.at[1]), source(zz, kk), dz + dk == 0)

    grads_of(4)
    grads_of(5)
    collect(2)
    reduce_1(2)
    query_back(2)
    reduce_3(0)
    grads_of(6)
    grads_of(7)
    collect(3)
    reduce_1(3)
    query_back(3)
    reduce_3(1)
    reduce_2(2)
    reduce_2(3)
    reduce_4(0)
    reduce_4(1)
    reduce_3(2)
    reduce_3(3)

    @pl.when(live_cols)
    def _():
        wait_bytes(dr, db_sem.at[1])
        for h in range(16):
            wide = dr[h].astype(F32)
            for half in range(2):
                df[half, pl.ds(h * 64, 64)] = wide[:, half * 128 : half * 128 + 128]

        def step(r, acc):
            left = jnp.concatenate([df[half, pl.ds(r, 16, stride=64)] for half in range(2)], axis=1)
            return acc + dot(left.astype(BF16), n_ref[r])

        ra[y * 4 + x] = lax.fori_loop(0, 64, step, jnp.zeros((16, 128), F32), unroll=8)

    @pl.when(cidx == 7)
    def _():
        ra[y * 4 + x] = jnp.zeros((16, 128), F32)

    for dy in range(4):
        for dx in range(4):
            if dy or dx:
                mine = ra.at[y * 4 + x]
                rcopy(mine, mine, ar_sem.at[0], ar_sem.at[1], there(dx, dy)).start()
    reduce_4(2)
    reduce_4(3)
    wait_bytes(ra.at[pl.ds(0, 15)], ar_sem.at[1])
    total = ra[0]
    for i in range(1, 16):
        total += ra[i]
    mine = rb.at[key * 8 + z]
    mine[...] = total
    for dz in range(8):
        for dk in range(2):
            if dz or dk:
                rcopy(
                    mine, mine, ar_sem.at[2], ar_sem.at[3], dev(x, y, rem(z + dz, 8), rem(key + dk, 2))
                ).start()

    wait_bytes(ob, ob_sem.at[1])
    for a in range(3):
        o_ref[a] = ob[:, a].reshape(8 * DH, 128).astype(F32).T.astype(BF16)

    wait_bytes(rb.at[pl.ds(0, 15)], ar_sem.at[3])
    summed = rb[0]
    for i in range(1, 16):
        summed += rb[i]
    sum_ref[...] = summed

    def sent(count):
        wait_bytes(skv.at[pl.ds(0, count)], kv_send)
        wait_bytes(sqd.at[pl.ds(0, count)], qd_sem.at[0])
        wait_bytes(ob.at[pl.ds(0, count)], ob_sem.at[0])

        @pl.when(live_cols)
        def _():
            wait_bytes(bs.at[:, pl.ds(0, count + 8)], bias_sem.at[0])
            wait_bytes(dbs.at[pl.ds(0, count + 6)], db_sem.at[0])

        @pl.when(cidx == 7)
        def _():
            wait_bytes(dbs.at[pl.ds(0, 14)], db_sem.at[0])

    @pl.when(same)
    def _():
        sent(7)

    @pl.when(jnp.logical_not(same))
    def _():
        sent(8)

    for c in range(CHUNKS):
        wait_bytes(blocks(15), ag_send.at[c])
        reduce_end(c)
    wait_bytes(ra.at[pl.ds(0, 15)], ar_sem.at[0])
    wait_bytes(rb.at[pl.ds(0, 15)], ar_sem.at[2])


def fused(rows, pair_feats, weight_t, gain, counts):
    vmem = pl.BlockSpec(memory_space=pltpu.VMEM)
    scratch = [
        pltpu.VMEM((64, 256, 128), BF16),
        pltpu.VMEM((8, 2, DH, 128), BF16),
        pltpu.VMEM((8, 2, DH, 128), BF16),
        pltpu.VMEM((4, 4, 4, 2, 2, DH, 128), BF16),
        pltpu.VMEM((4, 2, 2, DH, 128), BF16),
        pltpu.VMEM((2, 256, 128), F32),
        pltpu.VMEM((4, 16, 16, 256), BF16),
        pltpu.VMEM((ROWS, LIVE), BF16),
        pltpu.VMEM((ROWS, LIVE), F32),
        pltpu.VMEM((8, 2, DH, LIVE), BF16),
        pltpu.VMEM((8, 2, DH, 128), BF16),
        pltpu.VMEM((2, ROWS, LIVE), F32),
        pltpu.VMEM((2, ROWS, LIVE), F32),
        pltpu.VMEM((4, ROWS, LIVE), BF16),
        pltpu.VMEM((4, ROWS, LIVE), BF16),
        pltpu.VMEM((ROWS, LIVE), F32),
        pltpu.VMEM((2, 2, DH, LIVE), F32),
        pltpu.VMEM((2, DH, 128), F32),
        pltpu.VMEM((4, 4, 4, 2, 2, DH, 128), BF16),
        pltpu.VMEM((4, 2, DH, 128), BF16),
        pltpu.VMEM((4, 2, 4, 2, 2, DH, 128), BF16),
        pltpu.VMEM((4, 2, 3, 2, 2, DH, 128), BF16),
        pltpu.VMEM((4, 4, 2, 2, DH, 128), BF16),
        pltpu.VMEM((4, 2, 2, DH, 128), BF16),
        pltpu.VMEM((8, 3, DH, 128), BF16),
        pltpu.VMEM((16, 64, 256), BF16),
        pltpu.VMEM((16, 64, 256), BF16),
        pltpu.VMEM((2, 1024, 128), F32),
        pltpu.VMEM((16, 16, 128), F32),
        pltpu.VMEM((16, 16, 128), F32),
        pltpu.SemaphoreType.DMA((4,)),
        pltpu.SemaphoreType.DMA,
        pltpu.SemaphoreType.DMA((4,)),
        pltpu.SemaphoreType.DMA((2,)),
        pltpu.SemaphoreType.DMA((2,)),
        pltpu.SemaphoreType.DMA((4,)),
        pltpu.SemaphoreType.DMA((4, 4, 4)),
        pltpu.SemaphoreType.DMA((4, 3)),
        pltpu.SemaphoreType.DMA((4, 3)),
        pltpu.SemaphoreType.DMA((2,)),
        pltpu.SemaphoreType.DMA((2,)),
        pltpu.SemaphoreType.DMA((4,)),
    ]
    return pl.pallas_call(
        kernel,
        out_shape=(
            jax.ShapeDtypeStruct((3, 128, 8 * DH), BF16),
            jax.ShapeDtypeStruct((16, 128), F32),
        ),
        in_specs=[vmem, vmem, vmem, vmem, pl.BlockSpec(memory_space=pl.ANY), vmem, vmem, vmem],
        out_specs=(vmem, vmem),
        scratch_shapes=scratch,
        compiler_params=pltpu.CompilerParams(
            collective_id=0, has_side_effects=True, vmem_limit_bytes=56 * 1024 * 1024
        ),
    )(*rows, pair_feats, weight_t, gain, counts)


def finish(o_ref, sum_ref, wt_ref, gain_ref, key_ref, value_ref, query_ref, wg_ref, gg_ref):
    for a, ref in enumerate((key_ref, value_ref, query_ref)):
        whole = o_ref[a].astype(F32)
        ref[...] = jnp.stack([whole[:64], whole[64:]], axis=1).astype(BF16)
    summed = sum_ref[...]
    wg_ref[...] = summed * gain_ref[...]
    gg_ref[...] = jnp.sum(summed * wt_ref[...].astype(F32), axis=0, keepdims=True)


def local(
    query_proj, key_proj, value_proj, grad_out, pair_feats, pair_gain, bias_weight, atom_counts
):
    gain, weight_t = pair_gain[None], bias_weight.T
    out, summed = fused(
        (key_proj, value_proj, query_proj, grad_out), pair_feats, weight_t, gain, atom_counts[None]
    )
    vmem = pl.BlockSpec(memory_space=pltpu.VMEM)
    tokens = jax.ShapeDtypeStruct(query_proj.shape, BF16)
    key_grad, value_grad, query_grad, weight_grad, gain_grad = pl.pallas_call(
        finish,
        out_shape=(
            tokens,
            tokens,
            tokens,
            jax.ShapeDtypeStruct((16, 128), F32),
            jax.ShapeDtypeStruct((1, 128), F32),
        ),
        in_specs=[vmem] * 4,
        out_specs=(vmem,) * 5,
    )(out, summed, weight_t, gain)
    return query_grad, key_grad, value_grad, weight_grad.T, gain_grad[0]


def solution(mesh):
    tokens = P("qry", "smp", "key")
    return jax.shard_map(
        local,
        mesh=mesh,
        in_specs=(tokens, tokens, tokens, tokens, P("qry", ("smp", "key"), None), P(), P(), P()),
        out_specs=(tokens, tokens, tokens, P(), P()),
        check_vma=False,
    )
```

```python
import jax
import jax.numpy as jnp
from jax import lax
from jax.experimental import pallas as pl
from jax.experimental.pallas import tpu as pltpu
from jax.sharding import PartitionSpec as P

DH = 48
HEADS = 16
TOKENS = 2048
LIVE = 1792
ROWS = 128
CHUNKS = 4
PAIRS = 14
FACTOR = DH ** (-0.5)
LOG2E = 1.4426950408889634
MESH = pl.DeviceIdType.MESH
F32 = jnp.float32
BF16 = jnp.bfloat16


def rem(a, b):
    return lax.rem(a, jnp.int32(b))


def div(a, b):
    return lax.div(a, jnp.int32(b))


def dot(a, b):
    return jnp.dot(a, b, preferred_element_type=F32)


def dot_nt(a, b):
    return lax.dot_general(a, b, (((1,), (1,)), ((), ())), preferred_element_type=F32)


def wait_bytes(ref, sem):
    pltpu.make_async_copy(ref, ref, sem).wait()


def kernel(
    ak_ref, av_ref, aq_ref, ag_ref, x_ref, wt_ref, gain_ref, ac_ref,
    o_ref, sum_ref,
    n_ref, skv, sqd, g_ref, r_ref, bsf, bs, br, bf,
    kvt, qdt, s_ref, p_ref, w_ref, ds_ref, db, dkv, dq, d_ref, qb,
    e_ref, f_ref, h_ref, fb, ob, dbs, dr, df, ra, rb,
    x_sem, kv_send, kv_recv, qd_sem, bias_sem, ag_send, ag_recv,
    rs_send, rs_recv, ob_sem, db_sem, ar_sem,
):
    smp = lax.axis_index("smp")
    qry = lax.axis_index("qry")
    key = lax.axis_index("key")
    y = div(qry, 8)
    zh = rem(div(qry, 4), 2)
    x = rem(qry, 4)
    z = zh * 4 + smp
    cidx = smp * 2 + key
    lx = rem(x, 2)
    vx = x - lx + key
    vx2 = rem(vx + 2, 4)
    sx = x - lx + 1 - key
    sx2 = rem(sx + 2, 4)
    head = lx * 8 + z
    same = key == lx
    live_cols = cidx < 7

    def dev(xx, yy, zz, kk):
        return (rem(zz, 4), yy * 8 + div(zz, 4) * 4 + xx, kk)

    def rcopy(src, dst, send, recv, device):
        return pltpu.make_async_remote_copy(
            src_ref=src, dst_ref=dst, send_sem=send, recv_sem=recv, device_id=device, device_id_type=MESH
        )

    def owner(zz, half):
        return dev(x - lx + half, y, zz, lx)

    def source(zz, kk):
        return dev(vx, y, zz, kk)

    def there(dx, dy):
        return dev(rem(x + dx, 4), rem(y + dy, 4), z, key)

    sibling = dev(x, y, z, 1 - key)

    def send(src, dst, sems, device, first):
        if not first:
            rcopy(src, dst, sems[0], sems[1], device).start()
            return

        @pl.when(same)
        def _():
            pltpu.make_async_copy(src, dst, sems[1]).start()

        @pl.when(jnp.logical_not(same))
        def _():
            rcopy(src, dst, sems[0], sems[1], device).start()

    x_copies = [
        pltpu.make_async_copy(x_ref.at[pl.ds(16 * rc, 16)], n_ref.at[pl.ds(16 * rc, 16)], x_sem.at[rc])
        for rc in range(4)
    ]
    for copy in x_copies:
        copy.start()

    barrier = pltpu.get_barrier_semaphore()
    near = []
    for dz in range(8):
        for dx in range(2):
            for dk in range(2):
                if dz or dx or dk:
                    near.append(dev(x - lx + rem(lx + dx, 2), y, rem(z + dz, 8), rem(key + dk, 2)))
    for dy in range(4):
        for dx in range(4):
            if dy or dx == 2:
                near.append(there(dx, dy))
    near.append(dev(rem(x + 3 - 2 * lx, 4), y, z, key))
    for device in near:
        pl.semaphore_signal(barrier, inc=1, device_id=device, device_id_type=MESH)

    a_refs = (ak_ref, av_ref, aq_ref, ag_ref)

    def turned(a):
        whole = a_refs[a][...].astype(F32)
        return jnp.concatenate([whole[:, i] for i in range(2)], axis=0).T.astype(BF16).reshape(8, DH, 128)

    for a in range(2):
        skv[:, a] = turned(a)

    gw = wt_ref[...].astype(F32) * gain_ref[...]
    gw_high = gw.astype(BF16)
    gw_low = (gw - gw_high.astype(F32)).astype(BF16)
    gw_both = jnp.concatenate([gw_high, gw_low], axis=0)

    def bias_rows(rc):
        x_copies[rc].wait()

        def step(i, carry):
            row = rc * 16 + 2 * i
            tile = n_ref[pl.ds(row, 2)].reshape(512, 128)
            wide = tile.astype(F32)
            center = wide - jnp.mean(wide, axis=1, keepdims=True)
            spread = jnp.mean(center * center, axis=1, keepdims=True)
            normed = (center * lax.rsqrt(spread + 1e-05)).astype(BF16)
            n_ref[pl.ds(row, 2)] = normed.reshape(2, 256, 128)
            out = dot_nt(gw_both, normed)
            out = out[:16] + out[16:]
            for j in range(2):
                for half in range(2):
                    bsf[half, pl.ds((2 * i + j) * 16, 16)] = out[:, j * 256 + half * 128 : j * 256 + half * 128 + 128]
            return carry

        lax.fori_loop(0, 8, step, 0, unroll=4)
        for h in range(16):
            pieces = [bsf[half, pl.ds(h, 16, stride=16)] for half in range(2)]
            bs[rc, h] = jnp.concatenate(pieces, axis=1).astype(BF16)

    def bias_send(rc):
        @pl.when(live_cols)
        def _():
            dst = br.at[pl.ds(zh * 64 + 16 * rc, 16), pl.ds(pl.multiple_of(cidx * 256, 256), 256)]
            for dz in range(8):
                for dk in range(2):
                    zz, half = rem(z + dz, 8), rem(lx + dk, 2)
                    src = bs.at[rc, half * 8 + zz]
                    send(src, dst, (bias_sem.at[0], bias_sem.at[1]), owner(zz, half), dz + dk == 0)

    bias_rows(0)
    pl.semaphore_wait(barrier, len(near))

    for dz in range(8):
        zz = rem(z + dz, 8)
        send(skv.at[zz], g_ref.at[smp, y, x, zh], (kv_send, kv_recv.at[smp]), owner(zz, key), dz == 0)

    bias_send(0)
    for c in range(CHUNKS):
        d_ref[c, 3, :, 1] = jnp.zeros((4, 2, DH, 128), BF16)
    bias_rows(1)
    bias_send(1)

    def gather_send(c, yy, xx, device):
        ref = g_ref.at[c, yy, xx]
        rcopy(ref, ref, ag_send.at[c], ag_recv.at[c, yy, xx], device).start()

    def gather_wait(c, yy, xx):
        wait_bytes(g_ref.at[c, yy, xx], ag_recv.at[c, yy, xx])

    lines = [rem(y + dy, 4) for dy in range(4)]

    def gather_1(c):
        wait_bytes(g_ref.at[c, y, vx], kv_recv.at[c])
        gather_send(c, y, vx, there(2, 0))
        for dy in (1, 3, 2):
            gather_send(c, y, vx, there(0, dy))
        gather_send(c, y, vx, sibling)

    def gather_2(c):
        if c % 2 == 0:
            gather_wait(c, y, vx2)
            for dy in (1, 3, 2):
                gather_send(c, y, vx2, there(0, dy))
            gather_send(c, y, vx2, sibling)
        else:
            for dy in (1, 3, 2):
                gather_wait(c, lines[dy], vx)
                gather_send(c, lines[dy], vx, there(2, 0))
                gather_send(c, lines[dy], vx, sibling)

    def gather_3(c):
        if c % 2 == 0:
            for dy in (1, 3, 2):
                for xx in (vx, vx2):
                    gather_wait(c, lines[dy], xx)
                    gather_send(c, lines[dy], xx, sibling)
        else:
            for dy in (0, 1, 3, 2):
                gather_wait(c, lines[dy], vx2)
                gather_send(c, lines[dy], vx2, sibling)

    def gather_4(c):
        for yy in range(4):
            for xx in (sx, sx2):
                gather_wait(c, yy, xx)

    low_lanes = lax.broadcasted_iota(jnp.int32, (DH, 128), 1) < 64

    def merge(first, second):
        return (
            jnp.where(low_lanes, first, pltpu.roll(second, 64, 1)),
            jnp.where(low_lanes, pltpu.roll(first, 64, 1), second),
        )

    def tiles():
        for yy in range(4):
            for hi in range(2):
                for m in range(2):
                    if yy < 3 or hi == 0:
                        yield yy, hi, m, slice((yy * 4 + hi * 2 + m) * 128, (yy * 4 + hi * 2 + m + 1) * 128)

    def spread(c):
        for yy, hi, m, lanes in tiles():
            for a in range(2):
                both = merge(g_ref[c, yy, 2 * m, hi, a].astype(F32), g_ref[c, yy, 2 * m + 1, hi, a].astype(F32))
                for par in range(2):
                    kvt[2 * c + par, a, :, lanes] = both[par].astype(BF16)
        for a in range(2):
            both = merge(r_ref[c, 0, a].astype(F32), r_ref[c, 1, a].astype(F32))
            for par in range(2):
                qdt[2 * c + par, a] = both[par].astype(BF16)

    def scores_of(s):
        turned = [qdt[s, a].astype(F32).T.astype(BF16) for a in range(2)]
        s_ref[s % 2] = dot(turned[0], kvt[s, 0])
        p_ref[s % 2] = dot(turned[1], kvt[s, 1])

    def softmax_of(s):
        for g in range(8):
            at = slice(g * 16, g * 16 + 16)
            scores = s_ref[s % 2, at] * (FACTOR * LOG2E) + bf[at]
            top = jnp.max(scores, axis=1, keepdims=True)
            exponent = jnp.exp2(scores - top)
            slopes = p_ref[s % 2, at]
            total = jnp.sum(exponent, axis=1, keepdims=True)
            mixed = jnp.sum(exponent * slopes, axis=1, keepdims=True)
            inverse = 1.0 / total
            weights = exponent * inverse
            score_grad = weights * (slopes - mixed * inverse)
            w_ref[s, at] = weights.astype(BF16)
            ds_ref[s, at] = score_grad.astype(BF16)
            if s:
                db[at] += score_grad
            else:
                db[at] = score_grad

    def grads_of(s):
        dkv[s % 2, 0] = dot(qdt[s, 0], ds_ref[s])
        dkv[s % 2, 1] = dot(qdt[s, 1], w_ref[s])
        dq[s % 2] = dot_nt(kvt[s, 0], ds_ref[s]) * FACTOR

    def collect(c):
        for yy, hi, m, lanes in tiles():
            for a in range(2):
                both = merge(dkv[0, a, :, lanes], dkv[1, a, :, lanes])
                for e in range(2):
                    d_ref[c, yy, 2 * m + e, hi, a] = both[e].astype(BF16)
        both = merge(dq[0], dq[1])
        for hi in range(2):
            qb[c, hi] = both[hi].astype(BF16)

    def plus(ref, *others):
        total = ref[...].astype(F32)
        for other in others:
            total += other[...].astype(F32)
        return total

    def reduce_1(c):
        for j, xx in enumerate((sx, sx2)):
            rcopy(d_ref.at[c, :, xx], e_ref.at[c, j], rs_send.at[c, 0], rs_recv.at[c, 0], sibling).start()

    def reduce_2(c):
        wait_bytes(e_ref.at[c], rs_recv.at[c, 0])
        for j, xx in ((1, vx2), (0, vx)):
            for yy in range(4):
                ref = d_ref.at[c, yy, xx]
                ref[...] = plus(ref, e_ref.at[c, j, yy]).astype(BF16)
            if False and j:
                rcopy(d_ref.at[c, :, vx2], h_ref.at[c], rs_send.at[c, 1], rs_recv.at[c, 1], there(2, 0)).start()
        if True:
            for dy in (2, 1, 3):
                for j, xx in enumerate((vx, vx2)):
                    rcopy(
                        d_ref.at[c, lines[dy], xx], f_ref.at[c, j, dy - 1],
                        rs_send.at[c, 1], rs_recv.at[c, 1], there(0, dy),
                    ).start()

    def reduce_3(c):
        if True:
            wait_bytes(f_ref.at[c], rs_recv.at[c, 1])
            for j, xx in ((1, vx2), (0, vx)):
                ref = d_ref.at[c, y, xx]
                ref[...] = plus(ref, *(f_ref.at[c, j, i] for i in range(3))).astype(BF16)
                if j:
                    rcopy(ref, h_ref.at[c, 0], rs_send.at[c, 2], rs_recv.at[c, 2], there(2, 0)).start()
        else:
            wait_bytes(h_ref.at[c], rs_recv.at[c, 1])
            for dy in (2, 1, 3, 0):
                ref = d_ref.at[c, lines[dy], vx]
                ref[...] = plus(ref, h_ref.at[c, lines[dy]]).astype(BF16)
                if dy:
                    rcopy(
                        ref, f_ref.at[c, 0, dy - 1], rs_send.at[c, 2], rs_recv.at[c, 2], there(0, dy)
                    ).start()

    def reduce_4(c):
        if True:
            wait_bytes(h_ref.at[c, 0], rs_recv.at[c, 2])
            others = [h_ref.at[c, 0]]
        else:
            wait_bytes(f_ref.at[c, 0], rs_recv.at[c, 2])
            others = [f_ref.at[c, 0, i] for i in range(3)]
        for hi in range(2):
            for a in range(2):
                total = plus(d_ref.at[c, y, vx, hi, a], *(other.at[hi, a] for other in others))
                fb[c, hi, a] = (total * FACTOR if a == 0 else total).astype(BF16)
            back(fb.at[c, hi], c, hi, 0, 2)

    def back(src, c, hi, lo, count):
        zz = jnp.int32(4 * hi + c)
        dst = ob.at[z, pl.ds(lo, count)]
        here = jnp.logical_and(same, zz == z)

        @pl.when(here)
        def _():
            pltpu.make_async_copy(src, dst, ob_sem.at[1]).start()

        @pl.when(jnp.logical_not(here))
        def _():
            rcopy(src, dst, ob_sem.at[0], ob_sem.at[1], source(zz, lx)).start()

    def query_back(c):
        for hi in range(2):
            back(qb.at[c, pl.ds(hi, 1)], c, hi, 2, 1)

    def reduce_end(c):
        sizes = (8, 6, 1) if True else (8, 4, 3)
        for i, size in enumerate(sizes):
            wait_bytes(blocks(size), rs_send.at[c, i])

    def blocks(count):
        return n_ref.at[pl.ds(0, 3 * count), pl.ds(0, 64)]

    for c in range(CHUNKS):
        gather_1(c)
    for a in range(2):
        sqd[:, a] = turned(2 + a)
    for dz in range(8):
        zz = rem(z + dz, 8)
        send(sqd.at[zz], r_ref.at[smp, zh], (qd_sem.at[0], qd_sem.at[1]), owner(zz, key), dz == 0)
    bias_rows(2)
    bias_send(2)
    for c in range(2):
        gather_2(c)
    bias_rows(3)
    bias_send(3)
    for c in range(2, CHUNKS):
        gather_2(c)
    for c in range(2):
        gather_3(c)

    wait_bytes(r_ref, qd_sem.at[1])
    wait_bytes(br, bias_sem.at[1])
    mask = jnp.where(ac_ref[...] > 0, 0.0, -jnp.inf).astype(F32)
    for g in range(8):
        at = slice(g * 16, g * 16 + 16)
        bf[at] = (br[at].astype(F32) + mask[:, :LIVE]) * LOG2E

    def forward(c):
        gather_4(c)
        spread(c)
        scores_of(2 * c)
        scores_of(2 * c + 1)
        softmax_of(2 * c)
        softmax_of(2 * c + 1)

    def backward(c):
        grads_of(2 * c)
        grads_of(2 * c + 1)
        collect(c)
        reduce_1(c)

    forward(0)
    gather_3(2)
    backward(0)
    query_back(0)
    forward(1)
    gather_3(3)
    reduce_2(0)
    forward(2)
    forward(3)

    for hi in range(2):
        for col in range(7):
            dbs[hi * 8 + col] = db[hi * 64 : hi * 64 + 64, col * 256 : col * 256 + 256].astype(BF16)
    for dz in range(8):
        for dk in range(2):
            zz, kk = rem(z + dz, 8), rem(key + dk, 2)
            target = rem(zz, 4) * 2 + kk
            src = dbs.at[div(zz, 4) * 8 + target]

            @pl.when(target < 7)
            def _():
                send(src, dr.at[head], (db_sem.at[0], db_sem.at[1]), source(zz, kk), dz + dk == 0)

    backward(1)
    reduce_3(0)
    query_back(1)
    backward(2)
    reduce_2(1)
    query_back(2)
    backward(3)
    reduce_2(2)
    reduce_4(0)
    reduce_3(1)
    reduce_2(3)
    query_back(3)
    reduce_3(2)
    reduce_4(1)

    @pl.when(live_cols)
    def _():
        wait_bytes(dr, db_sem.at[1])
        for h in range(16):
            wide = dr[h].astype(F32)
            for half in range(2):
                df[half, pl.ds(h * 64, 64)] = wide[:, half * 128 : half * 128 + 128]

        def step(r, acc):
            left = jnp.concatenate([df[half, pl.ds(r, 16, stride=64)] for half in range(2)], axis=1)
            return acc + dot(left.astype(BF16), n_ref[r])

        ra[key * 8 + z] = lax.fori_loop(0, 64, step, jnp.zeros((16, 128), F32), unroll=8)

    @pl.when(cidx == 7)
    def _():
        ra[key * 8 + z] = jnp.zeros((16, 128), F32)

    mine = ra.at[key * 8 + z]
    for dz in range(8):
        for dk in range(2):
            if dz or dk:
                rcopy(
                    mine, mine, ar_sem.at[0], ar_sem.at[1], dev(x, y, rem(z + dz, 8), rem(key + dk, 2))
                ).start()
    reduce_3(3)
    reduce_4(2)
    reduce_4(3)
    wait_bytes(ra.at[pl.ds(0, 15)], ar_sem.at[1])
    total = ra[0]
    for i in range(1, 16):
        total += ra[i]
    last = rb.at[y * 4 + x]
    last[...] = total
    for dy in range(4):
        for dx in range(4):
            if dy or dx:
                rcopy(last, last, ar_sem.at[2], ar_sem.at[3], there(dx, dy)).start()

    wait_bytes(ob, ob_sem.at[1])
    for a in range(3):
        o_ref[a] = ob[:, a].reshape(8 * DH, 128).astype(F32).T.astype(BF16)

    wait_bytes(rb.at[pl.ds(0, 15)], ar_sem.at[3])
    summed = rb[0]
    for i in range(1, 16):
        summed += rb[i]
    sum_ref[...] = summed

    def sent(count):
        wait_bytes(skv.at[pl.ds(0, count)], kv_send)
        wait_bytes(sqd.at[pl.ds(0, count)], qd_sem.at[0])
        wait_bytes(ob.at[pl.ds(0, count)], ob_sem.at[0])

        @pl.when(live_cols)
        def _():
            wait_bytes(bs.at[:, pl.ds(0, count + 8)], bias_sem.at[0])
            wait_bytes(dbs.at[pl.ds(0, count + 6)], db_sem.at[0])

        @pl.when(cidx == 7)
        def _():
            wait_bytes(dbs.at[pl.ds(0, 14)], db_sem.at[0])

    @pl.when(same)
    def _():
        sent(7)

    @pl.when(jnp.logical_not(same))
    def _():
        sent(8)

    for c in range(CHUNKS):
        wait_bytes(blocks(15), ag_send.at[c])
        reduce_end(c)
    wait_bytes(ra.at[pl.ds(0, 15)], ar_sem.at[0])
    wait_bytes(rb.at[pl.ds(0, 15)], ar_sem.at[2])


def fused(rows, pair_feats, weight_t, gain, counts):
    vmem = pl.BlockSpec(memory_space=pltpu.VMEM)
    scratch = [
        pltpu.VMEM((64, 256, 128), BF16),
        pltpu.VMEM((8, 2, DH, 128), BF16),
        pltpu.VMEM((8, 2, DH, 128), BF16),
        pltpu.VMEM((4, 4, 4, 2, 2, DH, 128), BF16),
        pltpu.VMEM((4, 2, 2, DH, 128), BF16),
        pltpu.VMEM((2, 256, 128), F32),
        pltpu.VMEM((4, 16, 16, 256), BF16),
        pltpu.VMEM((ROWS, LIVE), BF16),
        pltpu.VMEM((ROWS, LIVE), F32),
        pltpu.VMEM((8, 2, DH, LIVE), BF16),
        pltpu.VMEM((8, 2, DH, 128), BF16),
        pltpu.VMEM((2, ROWS, LIVE), F32),
        pltpu.VMEM((2, ROWS, LIVE), F32),
        pltpu.VMEM((8, ROWS, LIVE), BF16),
        pltpu.VMEM((8, ROWS, LIVE), BF16),
        pltpu.VMEM((ROWS, LIVE), F32),
        pltpu.VMEM((2, 2, DH, LIVE), F32),
        pltpu.VMEM((2, DH, 128), F32),
        pltpu.VMEM((4, 4, 4, 2, 2, DH, 128), BF16),
        pltpu.VMEM((4, 2, DH, 128), BF16),
        pltpu.VMEM((4, 2, 4, 2, 2, DH, 128), BF16),
        pltpu.VMEM((4, 2, 3, 2, 2, DH, 128), BF16),
        pltpu.VMEM((4, 4, 2, 2, DH, 128), BF16),
        pltpu.VMEM((4, 2, 2, DH, 128), BF16),
        pltpu.VMEM((8, 3, DH, 128), BF16),
        pltpu.VMEM((16, 64, 256), BF16),
        pltpu.VMEM((16, 64, 256), BF16),
        pltpu.VMEM((2, 1024, 128), F32),
        pltpu.VMEM((16, 16, 128), F32),
        pltpu.VMEM((16, 16, 128), F32),
        pltpu.SemaphoreType.DMA((4,)),
        pltpu.SemaphoreType.DMA,
        pltpu.SemaphoreType.DMA((4,)),
        pltpu.SemaphoreType.DMA((2,)),
        pltpu.SemaphoreType.DMA((2,)),
        pltpu.SemaphoreType.DMA((4,)),
        pltpu.SemaphoreType.DMA((4, 4, 4)),
        pltpu.SemaphoreType.DMA((4, 3)),
        pltpu.SemaphoreType.DMA((4, 3)),
        pltpu.SemaphoreType.DMA((2,)),
        pltpu.SemaphoreType.DMA((2,)),
        pltpu.SemaphoreType.DMA((4,)),
    ]
    return pl.pallas_call(
        kernel,
        out_shape=(
            jax.ShapeDtypeStruct((3, 128, 8 * DH), BF16),
            jax.ShapeDtypeStruct((16, 128), F32),
        ),
        in_specs=[vmem, vmem, vmem, vmem, pl.BlockSpec(memory_space=pl.ANY), vmem, vmem, vmem],
        out_specs=(vmem, vmem),
        scratch_shapes=scratch,
        compiler_params=pltpu.CompilerParams(
            collective_id=0, has_side_effects=True, vmem_limit_bytes=56 * 1024 * 1024
        ),
    )(*rows, pair_feats, weight_t, gain, counts)


def finish(o_ref, sum_ref, wt_ref, gain_ref, key_ref, value_ref, query_ref, wg_ref, gg_ref):
    for a, ref in enumerate((key_ref, value_ref, query_ref)):
        whole = o_ref[a].astype(F32)
        ref[...] = jnp.stack([whole[:64], whole[64:]], axis=1).astype(BF16)
    summed = sum_ref[...]
    wg_ref[...] = summed * gain_ref[...]
    gg_ref[...] = jnp.sum(summed * wt_ref[...].astype(F32), axis=0, keepdims=True)


def local(
    query_proj, key_proj, value_proj, grad_out, pair_feats, pair_gain, bias_weight, atom_counts
):
    gain, weight_t = pair_gain[None], bias_weight.T
    out, summed = fused(
        (key_proj, value_proj, query_proj, grad_out), pair_feats, weight_t, gain, atom_counts[None]
    )
    vmem = pl.BlockSpec(memory_space=pltpu.VMEM)
    tokens = jax.ShapeDtypeStruct(query_proj.shape, BF16)
    key_grad, value_grad, query_grad, weight_grad, gain_grad = pl.pallas_call(
        finish,
        out_shape=(
            tokens,
            tokens,
            tokens,
            jax.ShapeDtypeStruct((16, 128), F32),
            jax.ShapeDtypeStruct((1, 128), F32),
        ),
        in_specs=[vmem] * 4,
        out_specs=(vmem,) * 5,
    )(out, summed, weight_t, gain)
    return query_grad, key_grad, value_grad, weight_grad.T, gain_grad[0]


def solution(mesh):
    tokens = P("qry", "smp", "key")
    return jax.shard_map(
        local,
        mesh=mesh,
        in_specs=(tokens, tokens, tokens, tokens, P("qry", ("smp", "key"), None), P(), P(), P()),
        out_specs=(tokens, tokens, tokens, P(), P()),
        check_vma=False,
    )
```

```python
import jax
import jax.numpy as jnp
from jax import lax
from jax.experimental import pallas as pl
from jax.experimental.pallas import tpu as pltpu
from jax.sharding import PartitionSpec as P

DH = 48
HEADS = 16
TOKENS = 2048
LIVE = 1792
ROWS = 128
CHUNKS = 4
PAIRS = 14
FACTOR = DH ** (-0.5)
LOG2E = 1.4426950408889634
MESH = pl.DeviceIdType.MESH
F32 = jnp.float32
BF16 = jnp.bfloat16


def rem(a, b):
    return lax.rem(a, jnp.int32(b))


def div(a, b):
    return lax.div(a, jnp.int32(b))


def dot(a, b):
    return jnp.dot(a, b, preferred_element_type=F32)


def dot_nt(a, b):
    return lax.dot_general(a, b, (((1,), (1,)), ((), ())), preferred_element_type=F32)


def wait_bytes(ref, sem):
    pltpu.make_async_copy(ref, ref, sem).wait()


def kernel(
    ak_ref, av_ref, aq_ref, ag_ref, x_ref, wt_ref, gain_ref, ac_ref,
    o_ref, sum_ref,
    n_ref, skv, sqd, g_ref, r_ref, bsf, bs, br, bf,
    kvt, qdt, s_ref, p_ref, w_ref, ds_ref, db, dkv, dq, d_ref, qb,
    e_ref, f_ref, h_ref, fb, ob, dbs, dr, df, ra, rb,
    x_sem, kv_send, kv_recv, qd_sem, bias_sem, ag_send, ag_recv,
    rs_send, rs_recv, ob_sem, db_sem, ar_sem,
):
    smp = lax.axis_index("smp")
    qry = lax.axis_index("qry")
    key = lax.axis_index("key")
    y = div(qry, 8)
    zh = rem(div(qry, 4), 2)
    x = rem(qry, 4)
    z = zh * 4 + smp
    cidx = smp * 2 + key
    lx = rem(x, 2)
    vx = x - lx + key
    vx2 = rem(vx + 2, 4)
    sx = x - lx + 1 - key
    sx2 = rem(sx + 2, 4)
    head = lx * 8 + z
    same = key == lx
    live_cols = cidx < 7

    def dev(xx, yy, zz, kk):
        return (rem(zz, 4), yy * 8 + div(zz, 4) * 4 + xx, kk)

    def rcopy(src, dst, send, recv, device):
        return pltpu.make_async_remote_copy(
            src_ref=src, dst_ref=dst, send_sem=send, recv_sem=recv, device_id=device, device_id_type=MESH
        )

    def owner(zz, half):
        return dev(x - lx + half, y, zz, lx)

    def source(zz, kk):
        return dev(vx, y, zz, kk)

    def there(dx, dy):
        return dev(rem(x + dx, 4), rem(y + dy, 4), z, key)

    sibling = dev(x, y, z, 1 - key)

    def send(src, dst, sems, device, first):
        if not first:
            rcopy(src, dst, sems[0], sems[1], device).start()
            return

        @pl.when(same)
        def _():
            pltpu.make_async_copy(src, dst, sems[1]).start()

        @pl.when(jnp.logical_not(same))
        def _():
            rcopy(src, dst, sems[0], sems[1], device).start()

    x_copies = [
        pltpu.make_async_copy(x_ref.at[pl.ds(16 * rc, 16)], n_ref.at[pl.ds(16 * rc, 16)], x_sem.at[rc])
        for rc in range(4)
    ]
    for copy in x_copies:
        copy.start()

    barrier = pltpu.get_barrier_semaphore()
    near = []
    for dz in range(8):
        for dx in range(2):
            for dk in range(2):
                if dz or dx or dk:
                    near.append(dev(x - lx + rem(lx + dx, 2), y, rem(z + dz, 8), rem(key + dk, 2)))
    for dy in range(4):
        for dx in range(4):
            if dy or dx == 2:
                near.append(there(dx, dy))
    near.append(dev(rem(x + 3 - 2 * lx, 4), y, z, key))
    for device in near:
        pl.semaphore_signal(barrier, inc=1, device_id=device, device_id_type=MESH)

    a_refs = (ak_ref, av_ref, aq_ref, ag_ref)

    def turned(a):
        whole = a_refs[a][...].astype(F32)
        return jnp.concatenate([whole[:, i] for i in range(2)], axis=0).T.astype(BF16).reshape(8, DH, 128)

    for a in range(2):
        skv[:, a] = turned(a)

    gw = wt_ref[...].astype(F32) * gain_ref[...]
    gw_high = gw.astype(BF16)
    gw_low = (gw - gw_high.astype(F32)).astype(BF16)
    gw_both = jnp.concatenate([gw_high, gw_low], axis=0)

    def bias_rows(rc):
        x_copies[rc].wait()

        def step(i, carry):
            row = rc * 16 + 2 * i
            tile = n_ref[pl.ds(row, 2)].reshape(512, 128)
            wide = tile.astype(F32)
            center = wide - jnp.mean(wide, axis=1, keepdims=True)
            spread = jnp.mean(center * center, axis=1, keepdims=True)
            normed = (center * lax.rsqrt(spread + 1e-05)).astype(BF16)
            n_ref[pl.ds(row, 2)] = normed.reshape(2, 256, 128)
            out = dot_nt(gw_both, normed)
            out = out[:16] + out[16:]
            for j in range(2):
                for half in range(2):
                    bsf[half, pl.ds((2 * i + j) * 16, 16)] = out[:, j * 256 + half * 128 : j * 256 + half * 128 + 128]
            return carry

        lax.fori_loop(0, 8, step, 0, unroll=4)
        for h in range(16):
            pieces = [bsf[half, pl.ds(h, 16, stride=16)] for half in range(2)]
            bs[rc, h] = jnp.concatenate(pieces, axis=1).astype(BF16)

    def bias_send(rc):
        @pl.when(live_cols)
        def _():
            dst = br.at[pl.ds(zh * 64 + 16 * rc, 16), pl.ds(pl.multiple_of(cidx * 256, 256), 256)]
            for dz in range(8):
                for dk in range(2):
                    zz, half = rem(z + dz, 8), rem(lx + dk, 2)
                    src = bs.at[rc, half * 8 + zz]
                    send(src, dst, (bias_sem.at[0], bias_sem.at[1]), owner(zz, half), dz + dk == 0)

    bias_rows(0)
    pl.semaphore_wait(barrier, len(near))

    for dz in range(8):
        zz = rem(z + dz, 8)
        send(skv.at[zz], g_ref.at[smp, y, x, zh], (kv_send, kv_recv.at[smp]), owner(zz, key), dz == 0)

    bias_send(0)
    for c in range(CHUNKS):
        d_ref[c, 3, :, 1] = jnp.zeros((4, 2, DH, 128), BF16)
    bias_rows(1)
    bias_send(1)

    def gather_send(c, yy, xx, device):
        ref = g_ref.at[c, yy, xx]
        rcopy(ref, ref, ag_send.at[c], ag_recv.at[c, yy, xx], device).start()

    def gather_wait(c, yy, xx):
        wait_bytes(g_ref.at[c, yy, xx], ag_recv.at[c, yy, xx])

    lines = [rem(y + dy, 4) for dy in range(4)]

    def gather_1(c):
        wait_bytes(g_ref.at[c, y, vx], kv_recv.at[c])
        gather_send(c, y, vx, there(2, 0))
        for dy in (1, 3, 2):
            gather_send(c, y, vx, there(0, dy))
        gather_send(c, y, vx, sibling)

    def gather_2(c):
        if c % 2 == 0:
            gather_wait(c, y, vx2)
            for dy in (1, 3, 2):
                gather_send(c, y, vx2, there(0, dy))
            gather_send(c, y, vx2, sibling)
        else:
            for dy in (1, 3, 2):
                gather_wait(c, lines[dy], vx)
                gather_send(c, lines[dy], vx, there(2, 0))
                gather_send(c, lines[dy], vx, sibling)

    def gather_3(c):
        if c % 2 == 0:
            for dy in (1, 3, 2):
                for xx in (vx, vx2):
                    gather_wait(c, lines[dy], xx)
                    gather_send(c, lines[dy], xx, sibling)
        else:
            for dy in (0, 1, 3, 2):
                gather_wait(c, lines[dy], vx2)
                gather_send(c, lines[dy], vx2, sibling)

    def gather_4(c):
        for yy in range(4):
            for xx in (sx, sx2):
                gather_wait(c, yy, xx)

    low_lanes = lax.broadcasted_iota(jnp.int32, (DH, 128), 1) < 64

    def merge(first, second):
        return (
            jnp.where(low_lanes, first, pltpu.roll(second, 64, 1)),
            jnp.where(low_lanes, pltpu.roll(first, 64, 1), second),
        )

    def tiles():
        for yy in range(4):
            for hi in range(2):
                for m in range(2):
                    if yy < 3 or hi == 0:
                        yield yy, hi, m, slice((yy * 4 + hi * 2 + m) * 128, (yy * 4 + hi * 2 + m + 1) * 128)

    def spread(c):
        for yy, hi, m, lanes in tiles():
            for a in range(2):
                both = merge(g_ref[c, yy, 2 * m, hi, a].astype(F32), g_ref[c, yy, 2 * m + 1, hi, a].astype(F32))
                for par in range(2):
                    kvt[2 * c + par, a, :, lanes] = both[par].astype(BF16)
        for a in range(2):
            both = merge(r_ref[c, 0, a].astype(F32), r_ref[c, 1, a].astype(F32))
            for par in range(2):
                qdt[2 * c + par, a] = both[par].astype(BF16)

    def scores_of(s):
        turned = [qdt[s, a].astype(F32).T.astype(BF16) for a in range(2)]
        s_ref[s % 2] = dot(turned[0], kvt[s, 0])
        p_ref[s % 2] = dot(turned[1], kvt[s, 1])

    def softmax_of(s):
        for g in range(8):
            at = slice(g * 16, g * 16 + 16)
            scores = s_ref[s % 2, at] * (FACTOR * LOG2E) + bf[at]
            top = jnp.max(scores, axis=1, keepdims=True)
            exponent = jnp.exp2(scores - top)
            slopes = p_ref[s % 2, at]
            total = jnp.sum(exponent, axis=1, keepdims=True)
            mixed = jnp.sum(exponent * slopes, axis=1, keepdims=True)
            inverse = 1.0 / total
            weights = exponent * inverse
            score_grad = weights * (slopes - mixed * inverse)
            w_ref[s, at] = weights.astype(BF16)
            ds_ref[s, at] = score_grad.astype(BF16)
            if s:
                db[at] += score_grad
            else:
                db[at] = score_grad

    def grads_of(s):
        dkv[s % 2, 0] = dot(qdt[s, 0], ds_ref[s])
        dkv[s % 2, 1] = dot(qdt[s, 1], w_ref[s])
        dq[s % 2] = dot_nt(kvt[s, 0], ds_ref[s]) * FACTOR

    def collect(c):
        for yy, hi, m, lanes in tiles():
            for a in range(2):
                both = merge(dkv[0, a, :, lanes], dkv[1, a, :, lanes])
                for e in range(2):
                    d_ref[c, yy, 2 * m + e, hi, a] = both[e].astype(BF16)
        both = merge(dq[0], dq[1])
        for hi in range(2):
            qb[c, hi] = both[hi].astype(BF16)

    def plus(ref, *others):
        total = ref[...].astype(F32)
        for other in others:
            total += other[...].astype(F32)
        return total

    def reduce_1(c):
        for j, xx in enumerate((sx, sx2)):
            rcopy(d_ref.at[c, :, xx], e_ref.at[c, j], rs_send.at[c, 0], rs_recv.at[c, 0], sibling).start()

    def reduce_2(c):
        wait_bytes(e_ref.at[c], rs_recv.at[c, 0])
        for j, xx in ((1, vx2), (0, vx)):
            for yy in range(4):
                ref = d_ref.at[c, yy, xx]
                ref[...] = plus(ref, e_ref.at[c, j, yy]).astype(BF16)
            if False and j:
                rcopy(d_ref.at[c, :, vx2], h_ref.at[c], rs_send.at[c, 1], rs_recv.at[c, 1], there(2, 0)).start()
        if True:
            for dy in (2, 1, 3):
                for j, xx in enumerate((vx, vx2)):
                    rcopy(
                        d_ref.at[c, lines[dy], xx], f_ref.at[c, j, dy - 1],
                        rs_send.at[c, 1], rs_recv.at[c, 1], there(0, dy),
                    ).start()

    def reduce_3(c):
        if True:
            wait_bytes(f_ref.at[c], rs_recv.at[c, 1])
            for j, xx in ((1, vx2), (0, vx)):
                ref = d_ref.at[c, y, xx]
                ref[...] = plus(ref, *(f_ref.at[c, j, i] for i in range(3))).astype(BF16)
                if j:
                    rcopy(ref, h_ref.at[c, 0], rs_send.at[c, 2], rs_recv.at[c, 2], there(2, 0)).start()
        else:
            wait_bytes(h_ref.at[c], rs_recv.at[c, 1])
            for dy in (2, 1, 3, 0):
                ref = d_ref.at[c, lines[dy], vx]
                ref[...] = plus(ref, h_ref.at[c, lines[dy]]).astype(BF16)
                if dy:
                    rcopy(
                        ref, f_ref.at[c, 0, dy - 1], rs_send.at[c, 2], rs_recv.at[c, 2], there(0, dy)
                    ).start()

    def reduce_4(c):
        if True:
            wait_bytes(h_ref.at[c, 0], rs_recv.at[c, 2])
            others = [h_ref.at[c, 0]]
        else:
            wait_bytes(f_ref.at[c, 0], rs_recv.at[c, 2])
            others = [f_ref.at[c, 0, i] for i in range(3)]
        for hi in range(2):
            for a in range(2):
                total = plus(d_ref.at[c, y, vx, hi, a], *(other.at[hi, a] for other in others))
                fb[c, hi, a] = (total * FACTOR if a == 0 else total).astype(BF16)
            back(fb.at[c, hi], c, hi, 0, 2)

    def back(src, c, hi, lo, count):
        zz = jnp.int32(4 * hi + c)
        dst = ob.at[z, pl.ds(lo, count)]
        here = jnp.logical_and(same, zz == z)

        @pl.when(here)
        def _():
            pltpu.make_async_copy(src, dst, ob_sem.at[1]).start()

        @pl.when(jnp.logical_not(here))
        def _():
            rcopy(src, dst, ob_sem.at[0], ob_sem.at[1], source(zz, lx)).start()

    def query_back(c):
        for hi in range(2):
            back(qb.at[c, pl.ds(hi, 1)], c, hi, 2, 1)

    def reduce_end(c):
        sizes = (8, 6, 1) if True else (8, 4, 3)
        for i, size in enumerate(sizes):
            wait_bytes(blocks(size), rs_send.at[c, i])

    def blocks(count):
        return n_ref.at[pl.ds(0, 3 * count), pl.ds(0, 64)]

    for c in range(CHUNKS):
        gather_1(c)
    for a in range(2):
        sqd[:, a] = turned(2 + a)
    for dz in range(8):
        zz = rem(z + dz, 8)
        send(sqd.at[zz], r_ref.at[smp, zh], (qd_sem.at[0], qd_sem.at[1]), owner(zz, key), dz == 0)
    bias_rows(2)
    bias_send(2)
    for c in range(2):
        gather_2(c)
    bias_rows(3)
    bias_send(3)
    for c in range(2, CHUNKS):
        gather_2(c)
    for c in range(2):
        gather_3(c)

    wait_bytes(r_ref, qd_sem.at[1])
    wait_bytes(br, bias_sem.at[1])
    mask = jnp.where(ac_ref[...] > 0, 0.0, -jnp.inf).astype(F32)
    for g in range(8):
        at = slice(g * 16, g * 16 + 16)
        bf[at] = (br[at].astype(F32) + mask[:, :LIVE]) * LOG2E

    def forward(c):
        gather_4(c)
        spread(c)
        scores_of(2 * c)
        scores_of(2 * c + 1)
        softmax_of(2 * c)
        softmax_of(2 * c + 1)

    def backward(c):
        grads_of(2 * c)
        grads_of(2 * c + 1)
        collect(c)
        reduce_1(c)

    forward(0)
    gather_3(2)
    backward(0)
    query_back(0)
    forward(1)
    gather_3(3)
    reduce_2(0)
    forward(2)
    forward(3)

    for hi in range(2):
        for col in range(7):
            dbs[hi * 8 + col] = db[hi * 64 : hi * 64 + 64, col * 256 : col * 256 + 256].astype(BF16)
    for dz in range(8):
        for dk in range(2):
            zz, kk = rem(z + dz, 8), rem(key + dk, 2)
            target = rem(zz, 4) * 2 + kk
            src = dbs.at[div(zz, 4) * 8 + target]

            @pl.when(target < 7)
            def _():
                send(src, dr.at[head], (db_sem.at[0], db_sem.at[1]), source(zz, kk), dz + dk == 0)

    backward(1)
    reduce_3(0)
    query_back(1)
    backward(2)
    reduce_2(1)
    query_back(2)
    backward(3)
    reduce_2(2)
    reduce_4(0)
    reduce_3(1)
    reduce_2(3)
    query_back(3)

    @pl.when(live_cols)
    def _():
        wait_bytes(dr, db_sem.at[1])
        for h in range(16):
            wide = dr[h].astype(F32)
            for half in range(2):
                df[half, pl.ds(h * 64, 64)] = wide[:, half * 128 : half * 128 + 128]

        def step(r, acc):
            left = jnp.concatenate([df[half, pl.ds(r, 16, stride=64)] for half in range(2)], axis=1)
            return acc + dot(left.astype(BF16), n_ref[r])

        ra[key * 8 + z] = lax.fori_loop(0, 64, step, jnp.zeros((16, 128), F32), unroll=8)

    @pl.when(cidx == 7)
    def _():
        ra[key * 8 + z] = jnp.zeros((16, 128), F32)

    mine = ra.at[key * 8 + z]
    for dz in range(8):
        for dk in range(2):
            if dz or dk:
                rcopy(
                    mine, mine, ar_sem.at[0], ar_sem.at[1], dev(x, y, rem(z + dz, 8), rem(key + dk, 2))
                ).start()
    reduce_3(2)
    reduce_3(3)
    reduce_4(1)
    reduce_4(2)
    reduce_4(3)
    wait_bytes(ra.at[pl.ds(0, 15)], ar_sem.at[1])
    total = ra[0]
    for i in range(1, 16):
        total += ra[i]
    last = rb.at[y * 4 + x]
    last[...] = total
    for dy in range(4):
        for dx in range(4):
            if dy or dx:
                rcopy(last, last, ar_sem.at[2], ar_sem.at[3], there(dx, dy)).start()

    wait_bytes(ob, ob_sem.at[1])
    for a in range(3):
        o_ref[a] = ob[:, a].reshape(8 * DH, 128).astype(F32).T.astype(BF16)

    wait_bytes(rb.at[pl.ds(0, 15)], ar_sem.at[3])
    summed = rb[0]
    for i in range(1, 16):
        summed += rb[i]
    sum_ref[...] = summed

    def sent(count):
        wait_bytes(skv.at[pl.ds(0, count)], kv_send)
        wait_bytes(sqd.at[pl.ds(0, count)], qd_sem.at[0])
        wait_bytes(ob.at[pl.ds(0, count)], ob_sem.at[0])

        @pl.when(live_cols)
        def _():
            wait_bytes(bs.at[:, pl.ds(0, count + 8)], bias_sem.at[0])
            wait_bytes(dbs.at[pl.ds(0, count + 6)], db_sem.at[0])

        @pl.when(cidx == 7)
        def _():
            wait_bytes(dbs.at[pl.ds(0, 14)], db_sem.at[0])

    @pl.when(same)
    def _():
        sent(7)

    @pl.when(jnp.logical_not(same))
    def _():
        sent(8)

    for c in range(CHUNKS):
        wait_bytes(blocks(15), ag_send.at[c])
        reduce_end(c)
    wait_bytes(ra.at[pl.ds(0, 15)], ar_sem.at[0])
    wait_bytes(rb.at[pl.ds(0, 15)], ar_sem.at[2])


def fused(rows, pair_feats, weight_t, gain, counts):
    vmem = pl.BlockSpec(memory_space=pltpu.VMEM)
    scratch = [
        pltpu.VMEM((64, 256, 128), BF16),
        pltpu.VMEM((8, 2, DH, 128), BF16),
        pltpu.VMEM((8, 2, DH, 128), BF16),
        pltpu.VMEM((4, 4, 4, 2, 2, DH, 128), BF16),
        pltpu.VMEM((4, 2, 2, DH, 128), BF16),
        pltpu.VMEM((2, 256, 128), F32),
        pltpu.VMEM((4, 16, 16, 256), BF16),
        pltpu.VMEM((ROWS, LIVE), BF16),
        pltpu.VMEM((ROWS, LIVE), F32),
        pltpu.VMEM((8, 2, DH, LIVE), BF16),
        pltpu.VMEM((8, 2, DH, 128), BF16),
        pltpu.VMEM((2, ROWS, LIVE), F32),
        pltpu.VMEM((2, ROWS, LIVE), F32),
        pltpu.VMEM((8, ROWS, LIVE), BF16),
        pltpu.VMEM((8, ROWS, LIVE), BF16),
        pltpu.VMEM((ROWS, LIVE), F32),
        pltpu.VMEM((2, 2, DH, LIVE), F32),
        pltpu.VMEM((2, DH, 128), F32),
        pltpu.VMEM((4, 4, 4, 2, 2, DH, 128), BF16),
        pltpu.VMEM((4, 2, DH, 128), BF16),
        pltpu.VMEM((4, 2, 4, 2, 2, DH, 128), BF16),
        pltpu.VMEM((4, 2, 3, 2, 2, DH, 128), BF16),
        pltpu.VMEM((4, 4, 2, 2, DH, 128), BF16),
        pltpu.VMEM((4, 2, 2, DH, 128), BF16),
        pltpu.VMEM((8, 3, DH, 128), BF16),
        pltpu.VMEM((16, 64, 256), BF16),
        pltpu.VMEM((16, 64, 256), BF16),
        pltpu.VMEM((2, 1024, 128), F32),
        pltpu.VMEM((16, 16, 128), F32),
        pltpu.VMEM((16, 16, 128), F32),
        pltpu.SemaphoreType.DMA((4,)),
        pltpu.SemaphoreType.DMA,
        pltpu.SemaphoreType.DMA((4,)),
        pltpu.SemaphoreType.DMA((2,)),
        pltpu.SemaphoreType.DMA((2,)),
        pltpu.SemaphoreType.DMA((4,)),
        pltpu.SemaphoreType.DMA((4, 4, 4)),
        pltpu.SemaphoreType.DMA((4, 3)),
        pltpu.SemaphoreType.DMA((4, 3)),
        pltpu.SemaphoreType.DMA((2,)),
        pltpu.SemaphoreType.DMA((2,)),
        pltpu.SemaphoreType.DMA((4,)),
    ]
    return pl.pallas_call(
        kernel,
        out_shape=(
            jax.ShapeDtypeStruct((3, 128, 8 * DH), BF16),
            jax.ShapeDtypeStruct((16, 128), F32),
        ),
        in_specs=[vmem, vmem, vmem, vmem, pl.BlockSpec(memory_space=pl.ANY), vmem, vmem, vmem],
        out_specs=(vmem, vmem),
        scratch_shapes=scratch,
        compiler_params=pltpu.CompilerParams(
            collective_id=0, has_side_effects=True, vmem_limit_bytes=56 * 1024 * 1024
        ),
    )(*rows, pair_feats, weight_t, gain, counts)


def finish(o_ref, sum_ref, wt_ref, gain_ref, key_ref, value_ref, query_ref, wg_ref, gg_ref):
    for a, ref in enumerate((key_ref, value_ref, query_ref)):
        whole = o_ref[a].astype(F32)
        ref[...] = jnp.stack([whole[:64], whole[64:]], axis=1).astype(BF16)
    summed = sum_ref[...]
    wg_ref[...] = summed * gain_ref[...]
    gg_ref[...] = jnp.sum(summed * wt_ref[...].astype(F32), axis=0, keepdims=True)


def local(
    query_proj, key_proj, value_proj, grad_out, pair_feats, pair_gain, bias_weight, atom_counts
):
    gain, weight_t = pair_gain[None], bias_weight.T
    out, summed = fused(
        (key_proj, value_proj, query_proj, grad_out), pair_feats, weight_t, gain, atom_counts[None]
    )
    vmem = pl.BlockSpec(memory_space=pltpu.VMEM)
    tokens = jax.ShapeDtypeStruct(query_proj.shape, BF16)
    key_grad, value_grad, query_grad, weight_grad, gain_grad = pl.pallas_call(
        finish,
        out_shape=(
            tokens,
            tokens,
            tokens,
            jax.ShapeDtypeStruct((16, 128), F32),
            jax.ShapeDtypeStruct((1, 128), F32),
        ),
        in_specs=[vmem] * 4,
        out_specs=(vmem,) * 5,
    )(out, summed, weight_t, gain)
    return query_grad, key_grad, value_grad, weight_grad.T, gain_grad[0]


def solution(mesh):
    tokens = P("qry", "smp", "key")
    return jax.shard_map(
        local,
        mesh=mesh,
        in_specs=(tokens, tokens, tokens, tokens, P("qry", ("smp", "key"), None), P(), P(), P()),
        out_specs=(tokens, tokens, tokens, P(), P()),
        check_vma=False,
    )
```
